128 devices in a mesh: tile: 64 (over x, z, y), win: 2 (over core).
Axes of the slice: x: 4, y: 4, z: 4, core: 2. Of those that a mesh axis runs over, the one named last changes fastest.
Arguments:
- grid: bfloat16 [2, 2048, 32, 256], P('win', 'tile'), may hold values from -6 to 6
- tokens: bfloat16 [2, 524288, 256], P('win', 'tile'), may hold values from -50 to 50
- targets: int32 [2, 4096, 1], P('win', 'tile'), may hold values from 0 to 63; in each aligned block of 64 rows (0 to 63, 64 to 127, ..., all dimensions but the last counted through in order) at most 2 rows name the same one
- sub_masks: int32 [2, 4096, 8], P('win', 'tile'), may hold values from 0 to 1, as said below
- live_counts: int32 [2, 4096], P('win', 'tile'), may hold values from 1 to 128
- edge_turns: int32 [64, 2], P('tile'), may hold values 0 or 1
- w_query: bfloat16 [256, 256], replicated, may hold values from -0.375 to 0.375
- w_key: bfloat16 [256, 256], replicated, may hold values from -0.375 to 0.375
- w_value: bfloat16 [256, 256], replicated, may hold values from -0.375 to 0.375
- w_out: bfloat16 [256, 256], replicated, may hold values from -0.375 to 0.375
- w_conv: bfloat16 [3, 3, 256, 256], replicated, may hold values from -0.21875 to 0.21875
- token_cotan: bfloat16 [2, 524288, 256], P('win', 'tile'), may hold values from -6 to 6
Outputs:
- token_out: bfloat16 [2, 524288, 256], P('win', 'tile')
- token_grad: bfloat16 [2, 524288, 256], P('win', 'tile')
- grid_grad: bfloat16 [2, 2048, 32, 256], P('win', 'tile')
- upd_query: float32 [256, 256], replicated
- upd_key: float32 [256, 256], replicated
- upd_value: float32 [256, 256], replicated
- upd_out: float32 [256, 256], replicated
- upd_conv: float32 [3, 3, 256, 256], replicated
The draws below stay inside these ranges and needn't reach their ends.
Inputs may be any that keep to these rules, and one draw needn't show every extreme that they name: `targets`: among the 64 token blocks of one device, no tile block is named more than 2 times, and some tile block is named exactly 2 times. `sub_masks`: each row holds exactly one 1.
All inputs are finite; a program needn't handle non-finite values. No bound on the sum of `edge_turns` on one device may be relied on, other than what follows from the above.
Results may differ from the reference program's by a relative error of at most 0.04.
The reference program's roundings to bfloat16 on the way count: a program that leaves them out, or rounds other values in their place, can miss the bound.
Values may be sent and summed in bfloat16 or wider, within the bound.
No kernel may reach another device: no remote copies, remote signals or barrier semaphores. Data moves between devices by JAX's collectives and lax.ppermute only.
A program may use at most 256 MiB of HBM per device.

```python
import math
import jax
import jax.numpy as jnp
import numpy as np
from jax import lax

D = 256
HEADS = 8
BT = 128
RY = 32
RX = 32
SUB = 8
KEYS = 128
CAP = 2
BLK = 64
NWIN = 2
ROWS = 2048
NBLOCKS = 4096
TOKENS = 524288
N_TILE = 64


def draw_tokens(key, part):
    key = jax.random.fold_in(key, 3)
    base = jnp.clip(jax.random.normal(key, (NWIN, TOKENS, D), jnp.float32), -4.0, 4.0)
    return base.astype(jnp.bfloat16)


def draw_sub_masks(key, part):
    key = jax.random.fold_in(key, 5)
    which = jax.random.randint(key, (NWIN, NBLOCKS), 0, SUB)
    return (which[:, :, None] == jnp.arange(SUB)[None, None, :]).astype(jnp.int32)


def set_ends(values, stream_key, least, top_value):
    longest = values.shape.index(max(values.shape))
    spots = []
    for shift in (0, 1):
        where = [jax.random.randint(jax.random.fold_in(stream_key, axis), (), 0, length) for axis, length in enumerate(values.shape)]
        where[longest] = (where[longest] + shift) % values.shape[longest]
        spots.append(tuple(where))
    return values.at[spots[0]].set(least).at[spots[1]].set(top_value)


def steps_of(rng, extent, pieces, least, high):
    def one(position, shards_of):
        steps = jax.random.uniform(jax.random.fold_in(jax.random.fold_in(rng, 6), position), (shards_of,), jnp.float32, least / len(pieces), high / len(pieces))
        return jnp.repeat(jnp.exp(steps), extent[position] // shards_of).reshape((-1,) + (1,) * (len(extent) - position - 1))

    gain = one(*pieces[0])
    for cut in pieces[1:]:
        gain = gain * one(*cut)
    return gain


def assign_block(rng, own, number, rows, number_of, top, bound, lean):
    sequence = jax.random.permutation(rng, number_of)
    heavy_load, common = shares(number_of, rows * top, bound, lean, True), shares(number_of, rows * top, bound, lean, False)
    places = jnp.arange(number_of)

    def named(lengths, rotation):
        used = int((lengths > 0).sum())
        fixed = max(1, used // 4)
        passed = fixed + (places - fixed + rotation * (used - fixed)) % max(1, number_of - fixed)
        return jnp.zeros((number_of,), jnp.int32).at[sequence[jnp.where(places < fixed, places, passed)]].set(jnp.asarray(lengths, jnp.int32))

    lengths = jnp.where(number % 4 == 0, named(heavy_load, number // 4), named(common, number - number // 4 - 1))
    mixed = jax.random.permutation(jax.random.fold_in(own, 3), number_of)
    giver, taker = mixed[0:number_of // 2 * 2:2], mixed[1:number_of // 2 * 2:2]
    slack = jnp.minimum(lengths[giver] - 1, bound - lengths[taker]) // 2
    slack = jnp.where((giver == sequence[0]) | (taker == sequence[0]) | (lengths[taker] == 0), 0, jnp.maximum(slack, 0))
    passed = jax.random.randint(jax.random.fold_in(own, 4), (number_of // 2,), 0, 1 << 20) % (slack + 1)
    lengths = lengths.at[giver].add(-passed).at[taker].add(passed)
    items = jnp.searchsorted(jnp.cumsum(lengths), jnp.arange(rows * top), side="right").astype(jnp.int32)
    listing = items.reshape(top, rows).T
    listing = listing[jax.random.permutation(jax.random.fold_in(own, 1), rows)]
    rotation = jax.random.randint(jax.random.fold_in(own, 2), (rows, 1), 0, top)
    return jnp.take_along_axis(listing, (jnp.arange(top)[None, :] + rotation) % top, axis=1)


def shares(number_of, total, limit, skew, full):
    portions = [(1 << 20) // math.isqrt(rank ** skew) + 1 for rank in range(1, number_of + 1)]
    largest = limit if full else min(limit, max(-(-total // number_of), total * portions[0] // sum(portions)))
    least = 1 if total - largest >= number_of - 1 else 0
    counts, surplus = [largest] + [least] * (number_of - 1), total - largest - least * (number_of - 1)
    while surplus > 0:
        movable = [i for i in range(1, number_of) if counts[i] < largest] or [i for i in range(1, number_of) if counts[i] < limit]
        mass, budget = sum([portions[i] for i in movable]), surplus
        for i in movable:
            more = min(limit - counts[i], max(1, budget * portions[i] // mass), surplus)
            counts[i] = counts[i] + more
            surplus = surplus - more
    return np.array(counts)


def gaussian(key, shape, deviation, bound, pieces=(), kind=jnp.bfloat16):
    gain = steps_of(key, shape, pieces, -0.22, 0.18) if pieces else 1.0
    result = jax.random.normal(key, shape, jnp.float32) * deviation * gain
    return jnp.minimum(jnp.maximum(result, -bound), bound).astype(kind)


def setup_inputs(seed: int = 0) -> dict:
    key_list = jax.random.split(jax.random.key(seed), 13)
    grid = gaussian(key_list[0], (NWIN, ROWS, RX, D), 1.0, 6.0, ((0, 2), (1, 64)))
    tokens = draw_tokens(jax.random.fold_in(key_list[12], 71), 0)
    targets_keys = jax.random.split(jax.random.fold_in(key_list[2], 1), NWIN * NBLOCKS // BLK)
    targets_turns = jax.random.permutation(jax.random.fold_in(key_list[2], 3), NWIN * NBLOCKS // BLK)
    targets = jax.vmap(lambda own, number: assign_block(jax.random.fold_in(key_list[2], 2), own, number, BLK, N_TILE, 1, CAP, 2))(targets_keys, targets_turns).reshape((NWIN, NBLOCKS, 1))
    sub_masks = draw_sub_masks(jax.random.fold_in(key_list[12], 71), 0)
    live_counts = set_ends(jax.random.randint(key_list[4], (NWIN, NBLOCKS), 1, BT + 1), jax.random.fold_in(key_list[4], 1), 1, BT).astype(jnp.int32)
    edge_turns = set_ends((jax.random.randint(key_list[5], (N_TILE, 2), 0, 2) < 1).astype(jnp.int32), jax.random.fold_in(key_list[5], 1), 0, 1)
    w_query = gaussian(key_list[6], (D, D), D ** -0.5, 0.375)
    w_key = gaussian(key_list[7], (D, D), D ** -0.5, 0.375)
    w_value = gaussian(key_list[8], (D, D), D ** -0.5, 0.375)
    w_out = gaussian(key_list[9], (D, D), D ** -0.5, 0.375)
    w_conv = gaussian(key_list[10], (3, 3, D, D), (3 * D) ** -0.5, 0.21875)
    token_cotan = gaussian(key_list[11], (NWIN, TOKENS, D), 1.0, 6.0, ((0, 2), (1, 64)))
    return {"grid": grid, "tokens": tokens, "targets": targets, "sub_masks": sub_masks, "live_counts": live_counts, "edge_turns": edge_turns, "w_query": w_query, "w_key": w_key, "w_value": w_value, "w_out": w_out, "w_conv": w_conv, "token_cotan": token_cotan}


EPSILON = 1e-06

def flip_rows(rows, flags):
    return jnp.where(flags[:, None, None] == 1, rows[:, ::-1], rows)

def scaled_update(grad):
    return grad / jnp.sqrt(jnp.mean(grad * grad) + EPSILON)

def reference(grid, tokens, targets, sub_masks, live_counts, edge_turns, w_query, w_key, w_value, w_out, w_conv, token_cotan):
    f32 = jnp.float32
    bf16 = jnp.bfloat16
    head_dim = D // HEADS
    scale = 1.0 / math.sqrt(head_dim)
    grad_query = jnp.zeros((D, D), f32)
    grad_key = jnp.zeros((D, D), f32)
    grad_value = jnp.zeros((D, D), f32)
    grad_out = jnp.zeros((D, D), f32)
    grad_conv = jnp.zeros((3, 3, D, D), f32)
    outs_list = []
    tgrad_list = []
    ggrad_list = []
    for window in range(NWIN):
        blocks = grid[window].reshape(N_TILE, RY, RX, D)
        above = flip_rows(jnp.roll(blocks[:, -1], 1, axis=0), edge_turns[:, 0])
        below = flip_rows(jnp.roll(blocks[:, 0], -1, axis=0), edge_turns[:, 1])
        rimmed = jnp.concatenate([above[:, None], blocks, below[:, None]], axis=1)
        rimmed = jnp.pad(rimmed, ((0, 0), (0, 0), (1, 1), (0, 0)))
        total = blocks.astype(f32)
        for a in range(3):
            for b in range(3):
                cells = rimmed[:, a:a + RY, b:b + RX].reshape(-1, D)
                total = total + jnp.dot(cells, w_conv[a, b], preferred_element_type=f32).reshape(N_TILE, RY, RX, D)
        hidden = total.astype(bf16).reshape(-1, D)
        grid_keys = jnp.dot(hidden, w_key, preferred_element_type=f32).astype(bf16)
        grid_values = jnp.dot(hidden, w_value, preferred_element_type=f32).astype(bf16)
        key_table = grid_keys.reshape(N_TILE * SUB, KEYS, D)
        value_table = grid_values.reshape(N_TILE * SUB, KEYS, D)
        x = tokens[window]
        queries = jnp.dot(x, w_query, preferred_element_type=f32).astype(bf16)
        which_sub = lax.optimization_barrier(jnp.sum(sub_masks[window] * jnp.arange(SUB, dtype=jnp.int32)[None, :], axis=1))
        picks = (targets[window, :, 0] * SUB + which_sub).astype(jnp.int32)
        live = (jnp.arange(BT, dtype=jnp.int32)[None, :] < live_counts[window][:, None]).reshape(-1, 1)
        query_groups = queries.reshape(N_TILE, BLK, BT, D)
        pick_groups = picks.reshape(N_TILE, BLK)

        def scored(q_g, p_g):
            k_h = key_table[p_g].astype(f32).reshape(BLK, KEYS, HEADS, head_dim)
            v_h = value_table[p_g].astype(f32).reshape(BLK, KEYS, HEADS, head_dim)
            q_h = q_g.astype(f32).reshape(BLK, BT, HEADS, head_dim)
            scores = jnp.einsum('nqhe,nkhe->nhqk', q_h, k_h) * scale
            weights = jax.nn.softmax(scores, axis=-1).astype(bf16)
            return (q_h, k_h, v_h, weights)

        def forward_group(item):
            q_g, p_g = item
            q_h, k_h, v_h, weights = scored(q_g, p_g)
            attended = jnp.einsum('nhqk,nkhe->nqhe', weights.astype(f32), v_h)
            return attended.astype(bf16).reshape(BLK, BT, D)
        attended = lax.map(forward_group, (query_groups, pick_groups)).reshape(-1, D)
        mixed = jnp.dot(attended, w_out, preferred_element_type=f32)
        outs_list.append(jnp.where(live, mixed, 0.0).astype(bf16))
        out_cot = jnp.where(live, token_cotan[window], jnp.zeros((), bf16))
        grad_out = grad_out + jnp.dot(attended.T, out_cot, preferred_element_type=f32)
        attended_grad = jnp.dot(out_cot, w_out.T, preferred_element_type=f32).astype(bf16)
        grad_groups = attended_grad.reshape(N_TILE, BLK, BT, D)

        def backward_group(carry, item):
            key_acc, value_acc = carry
            q_g, p_g, d_g = item
            q_h, k_h, v_h, weights = scored(q_g, p_g)
            d_h = d_g.astype(f32).reshape(BLK, BT, HEADS, head_dim)
            weight_grad = jnp.einsum('nqhe,nkhe->nhqk', d_h, v_h)
            wf = weights.astype(f32)
            score_grad = (wf * (weight_grad - lax.optimization_barrier(jnp.sum(wf * weight_grad, axis=-1, keepdims=True))) * scale).astype(bf16)
            sf = score_grad.astype(f32)
            query_grad = jnp.einsum('nhqk,nkhe->nqhe', sf, k_h).astype(bf16).reshape(BLK, BT, D)
            dk = jnp.einsum('nhqk,nqhe->nkhe', sf, q_h).reshape(BLK, KEYS, D)
            dv = jnp.einsum('nhqk,nqhe->nkhe', wf, d_h).reshape(BLK, KEYS, D)
            return ((key_acc.at[p_g].add(dk), value_acc.at[p_g].add(dv)), query_grad)
        zero = jnp.zeros((N_TILE * SUB, KEYS, D), f32)
        (key_grad, value_grad), query_grads = lax.scan(backward_group, (zero, zero), (query_groups, pick_groups, grad_groups))
        query_grad = query_grads.reshape(-1, D)
        tgrad_list.append(jnp.dot(query_grad, w_query.T, preferred_element_type=f32).astype(bf16))
        grad_query = grad_query + jnp.dot(x.T, query_grad, preferred_element_type=f32)
        keys_back = key_grad.reshape(-1, D).astype(bf16)
        values_back = value_grad.reshape(-1, D).astype(bf16)
        grad_key = grad_key + jnp.dot(hidden.T, keys_back, preferred_element_type=f32)
        grad_value = grad_value + jnp.dot(hidden.T, values_back, preferred_element_type=f32)
        hidden_grad = jnp.dot(keys_back, w_key.T, preferred_element_type=f32) + jnp.dot(values_back, w_value.T, preferred_element_type=f32)
        hidden_back = hidden_grad.astype(bf16)
        rim_grad = jnp.zeros((N_TILE, RY + 2, RX + 2, D), f32)
        tap_rows = []
        for a in range(3):
            for b in range(3):
                cells = rimmed[:, a:a + RY, b:b + RX].reshape(-1, D)
                tap_rows.append(jnp.dot(cells.T, hidden_back, preferred_element_type=f32))
                back = jnp.dot(hidden_back, w_conv[a, b].T, preferred_element_type=f32).reshape(N_TILE, RY, RX, D)
                rim_grad = rim_grad.at[:, a:a + RY, b:b + RX].add(back)
        grad_conv = grad_conv + jnp.stack(tap_rows).reshape(3, 3, D, D)
        field_grad = hidden_grad.reshape(N_TILE, RY, RX, D) + rim_grad[:, 1:-1, 1:-1]
        up_part = flip_rows(rim_grad[:, 0, 1:-1], edge_turns[:, 0])
        down_part = flip_rows(rim_grad[:, -1, 1:-1], edge_turns[:, 1])
        field_grad = field_grad.at[:, -1].add(jnp.roll(up_part, -1, axis=0))
        field_grad = field_grad.at[:, 0].add(jnp.roll(down_part, 1, axis=0))
        ggrad_list.append(field_grad.astype(bf16).reshape(ROWS, RX, D))
    token_out = jnp.stack(outs_list)
    token_grad = jnp.stack(tgrad_list)
    grid_grad = jnp.stack(ggrad_list)
    return (token_out, token_grad, grid_grad, scaled_update(grad_query), scaled_update(grad_key), scaled_update(grad_value), scaled_update(grad_out), scaled_update(grad_conv))
```

```python
import math

import jax
import jax.numpy as jnp
from jax import lax
from jax.experimental import pallas as pl
from jax.experimental.pallas import tpu as pltpu
from jax.sharding import PartitionSpec as P

D = 256
HEADS = 8
HD = 32
BT = 128
RY = 32
RX = 32
SUB = 8
KEYS = 128
CELLS = RY * RX
EPSILON = 1e-06
SCALE = 1.0 / math.sqrt(HD)
EXP2_SCALE = SCALE * math.log2(math.e)
STEP = 8

f32 = jnp.float32
bf16 = jnp.bfloat16


def mm(a, b):
    return lax.dot_general(a, b, (((1,), (0,)), ((), ())), preferred_element_type=f32)


def mm_nt(a, b):
    return lax.dot_general(a, b, (((1,), (1,)), ((), ())), preferred_element_type=f32)


def whole(shape):
    return pl.BlockSpec(shape, lambda *_: (0,) * len(shape))


def hidden_kernel(req_ref, rim_ref, w_ref, send_a, send_b, shifts_ref, hid, sems):
    rim = rim_ref[...].astype(f32)
    rows = rim.shape[0]
    col = lax.broadcasted_iota(jnp.int32, (rows, D), 0) % RX
    shifts_ref[0] = jnp.where(col == 0, 0.0, pltpu.roll(rim, 1, 0)).astype(bf16)
    shifts_ref[1] = rim_ref[...]
    shifts_ref[2] = jnp.where(col == RX - 1, 0.0, pltpu.roll(rim, rows - 1, 0)).astype(bf16)
    piece = CELLS // 4

    @pl.loop(0, 4)
    def _(i):
        base = i * piece
        total = rim_ref[pl.ds(pl.multiple_of(base + RX, RX), piece), :].astype(f32)
        for a in range(3):
            for b in range(3):
                cells = shifts_ref[b, pl.ds(pl.multiple_of(base + a * RX, RX), piece), :]
                total = total + mm(cells, w_ref[3 * a + b])
        hid[pl.ds(pl.multiple_of(base, piece), piece), :] = total.astype(bf16)

    count = send_a.shape[0]

    def copy(c, out, s):
        sub = jnp.minimum(req_ref[s, c], SUB - 1)
        source = hid.at[pl.ds(pl.multiple_of(sub * KEYS, KEYS), KEYS), :]
        return pltpu.make_async_copy(source, out.at[s], sems.at[c])

    @pl.loop(0, count)
    def _(s):
        copy(0, send_a, s).start()
        copy(1, send_b, s).start()

    @pl.loop(0, count)
    def _(s):
        copy(0, send_a, s).wait()
        copy(1, send_b, s).wait()


def hidden_sends(req, rimmed, w_conv):
    count = req.shape[0]
    slots = jax.ShapeDtypeStruct((count, KEYS, D), bf16)
    rows = (RY + 2) * RX
    return pl.pallas_call(
        hidden_kernel,
        out_shape=(slots, slots, jax.ShapeDtypeStruct((3, rows, D), bf16)),
        in_specs=[
            pl.BlockSpec(memory_space=pltpu.SMEM),
            pl.BlockSpec(memory_space=pltpu.VMEM),
            pl.BlockSpec(memory_space=pltpu.VMEM),
        ],
        out_specs=(
            pl.BlockSpec(memory_space=pl.ANY),
            pl.BlockSpec(memory_space=pl.ANY),
            pl.BlockSpec(memory_space=pltpu.VMEM),
        ),
        scratch_shapes=[
            pltpu.VMEM((CELLS, D), bf16),
            pltpu.SemaphoreType.DMA((2,)),
        ],
        compiler_params=pltpu.CompilerParams(vmem_limit_bytes=40 * 1024 * 1024),
        cost_estimate=pl.CostEstimate(
            flops=2 * 9 * CELLS * D * D, bytes_accessed=20_000_000, transcendentals=0
        ),
        name="conv_sends",
    )(req, rimmed, w_conv)


def attend_kernel(
    meta, h_ref, x_ref, c_ref, wq, wq_t, wkv, wkv_t, wo, wo_t, grads_in, *rest
):
    out_ref, tgrad_ref, hgrad_ref, grads_ref = rest[-4:]
    i = pl.program_id(0)

    @pl.when(i == 0)
    def _():
        grads_ref[...] = grads_in[...]

    @pl.when(i < meta[3, 0])
    def _():
        live = meta[2, i]
        h = h_ref[0]
        x = x_ref[0]
        row = lax.broadcasted_iota(jnp.int32, (BT, D), 0)
        cot = jnp.where(row < live, c_ref[0].astype(f32), 0.0).astype(bf16)
        kv = mm(h, wkv[...]).astype(bf16)
        kv_t = mm_nt(wkv_t[...], h).astype(bf16)
        q_t = mm_nt(wq_t[...], x).astype(bf16)
        d_t = mm_nt(wo[...], cot).astype(bf16)
        zero = jnp.zeros((HD, BT), bf16)
        none = jnp.zeros((2 * HD, 2 * BT), bf16)

        def paired(t, p):
            first = t[2 * HD * p : 2 * HD * p + HD]
            second = t[2 * HD * p + HD : 2 * HD * p + 2 * HD]
            return jnp.concatenate(
                [
                    jnp.concatenate([first, zero], axis=1),
                    jnp.concatenate([zero, second], axis=1),
                ],
                axis=0,
            )

        def deep(pair, p):
            return jnp.concatenate([pair, none] if p % 2 == 0 else [none, pair], axis=0)

        att_rows, qg_rows, kg_rows, vg_rows = [], [], [], []
        for p in range(HEADS // 2):
            lanes = slice(128 * (p // 2), 128 * (p // 2) + 128)
            feats = slice(2 * HD * p, 2 * HD * p + 2 * HD)
            q2 = paired(q_t, p)
            d2 = paired(d_t, p)
            scores = mm(kv[:, lanes], deep(q2, p))
            top = jnp.max(scores, axis=0, keepdims=True)
            e = jnp.exp2((scores - top) * EXP2_SCALE)
            w = (e * (1.0 / jnp.sum(e, axis=0, keepdims=True))).astype(bf16)
            wf = w.astype(f32)
            wg = mm(kv[:, D + lanes.start : D + lanes.stop], deep(d2, p))
            mean = jnp.sum(wf * wg, axis=0, keepdims=True)
            sg = (wf * (wg - mean)).astype(bf16)
            att = mm(kv_t[D + feats.start : D + feats.stop], w)
            att_rows += [att[:HD, :BT], att[HD:, BT:]]
            qg = mm(kv_t[feats], sg)
            qg_rows += [qg[:HD, :BT], qg[HD:, BT:]]
            kg_rows.append(mm_nt(q2, sg) * SCALE)
            vg_rows.append(mm_nt(d2, w))
        att_t = jnp.concatenate(att_rows, axis=0).astype(bf16)
        qg_t = (jnp.concatenate(qg_rows, axis=0) * SCALE).astype(bf16)
        kvg_t = jnp.concatenate(kg_rows + vg_rows, axis=0).astype(bf16)
        lane = lax.broadcasted_iota(jnp.int32, (D, BT), 1)
        mixed = jnp.where(lane < live, mm(wo_t[...], att_t), 0.0)
        out_ref[0] = mixed.T.astype(bf16)
        tgrad_ref[0] = mm(wq[...], qg_t).T.astype(bf16)
        hgrad_ref[0] = mm(wkv[...], kvg_t).astype(bf16)
        grads_ref[0:256] += mm(qg_t, x)
        grads_ref[256:768] += mm(kvg_t, h)
        grads_ref[768:1024] += mm(att_t, cot)


def attend(meta, slots, x, cot, weights, grads, kept):
    nblocks = x.shape[0]
    count = slots.shape[0]
    by_tile = lambda i, m: (m[1, i], 0, 0)
    by_block = lambda i, m: (m[0, i], 0, 0)
    rows = pl.BlockSpec((1, BT, D), by_block)
    in_specs = [pl.BlockSpec((1, KEYS, D), by_tile), rows, rows]
    in_specs += [whole(w.shape) for w in weights] + [whole((4 * D, D))]
    in_specs += [pl.BlockSpec(memory_space=pl.ANY)] * len(kept)
    args = [meta, slots, x, cot, *weights, grads, *kept]
    first_kept = len(args) - len(kept)
    token_shape = jax.ShapeDtypeStruct((nblocks, BT, D), bf16)
    return pl.pallas_call(
        attend_kernel,
        out_shape=(
            token_shape,
            token_shape,
            jax.ShapeDtypeStruct((count, D, KEYS), bf16),
            jax.ShapeDtypeStruct((4 * D, D), f32),
        ),
        grid_spec=pltpu.PrefetchScalarGridSpec(
            num_scalar_prefetch=1,
            grid=(nblocks,),
            in_specs=in_specs,
            out_specs=(
                rows,
                rows,
                pl.BlockSpec((1, D, KEYS), by_tile),
                whole((4 * D, D)),
            ),
        ),
        input_output_aliases={first_kept + j: j for j in range(len(kept))},
        compiler_params=pltpu.CompilerParams(
            dimension_semantics=("arbitrary",), vmem_limit_bytes=40 * 1024 * 1024
        ),
        cost_estimate=pl.CostEstimate(
            flops=nblocks * 400_000_000, bytes_accessed=nblocks * 400_000, transcendentals=0
        ),
        name="attend",
    )(*args)


def add_slots(req_ref, slots_ref, acc_ref, column):
    i = pl.program_id(0)
    for j in range(STEP):
        sub = req_ref[i * STEP + j, column]

        @pl.when(sub < SUB)
        def _():
            at = pl.ds(pl.multiple_of(sub * D, D), D)
            acc_ref[at, :] += slots_ref[j].astype(f32)


def gather_kernel(req_ref, slots_ref, acc_ref):
    @pl.when(pl.program_id(0) == 0)
    def _():
        acc_ref[...] = jnp.zeros_like(acc_ref)

    add_slots(req_ref, slots_ref, acc_ref, 0)


def finish_kernel(req_ref, slots_ref, acc_in, shifts_ref, grads_ref, hgrad_ref, sums_ref, acc_ref, back_t):
    i = pl.program_id(0)

    @pl.when(i == 0)
    def _():
        acc_ref[...] = acc_in[...]

    add_slots(req_ref, slots_ref, acc_ref, 1)

    @pl.when(i == pl.num_programs(0) - 1)
    def _():
        sums_ref[0 : 4 * D] = grads_ref[...].astype(bf16)
        for s in range(SUB):
            part = acc_ref[s * D : (s + 1) * D, :]
            hgrad_ref[s * KEYS : (s + 1) * KEYS, :] = part.T
            back_t[:, s * KEYS : (s + 1) * KEYS] = part.astype(bf16)
        for a in range(3):
            for b in range(3):
                at = (4 + 3 * a + b) * D
                cells = shifts_ref[b, a * RX : a * RX + CELLS, :]
                sums_ref[at : at + D] = mm(back_t[...], cells).astype(bf16)


def slot_specs(count):
    return [
        pl.BlockSpec(memory_space=pltpu.SMEM),
        pl.BlockSpec((STEP, D, KEYS), lambda i: (i, 0, 0)),
    ]


def gather_slots(req, slots):
    count = slots.shape[0]
    return pl.pallas_call(
        gather_kernel,
        out_shape=jax.ShapeDtypeStruct((SUB * D, KEYS), f32),
        grid=(count // STEP,),
        in_specs=slot_specs(count),
        out_specs=whole((SUB * D, KEYS)),
        compiler_params=pltpu.CompilerParams(vmem_limit_bytes=40 * 1024 * 1024),
        cost_estimate=pl.CostEstimate(
            flops=count * D * KEYS, bytes_accessed=count * D * KEYS * 2, transcendentals=0
        ),
        name="gather_slots",
    )(req, slots)


def finish(req, slots, acc, shifts, grads):
    count = slots.shape[0]
    return pl.pallas_call(
        finish_kernel,
        out_shape=(
            jax.ShapeDtypeStruct((CELLS, D), f32),
            jax.ShapeDtypeStruct((13 * D, D), bf16),
        ),
        grid=(count // STEP,),
        in_specs=slot_specs(count)
        + [whole(acc.shape), whole(shifts.shape), whole(grads.shape)],
        out_specs=(whole((CELLS, D)), whole((13 * D, D))),
        scratch_shapes=[
            pltpu.VMEM((SUB * D, KEYS), f32),
            pltpu.VMEM((D, CELLS), bf16),
        ],
        compiler_params=pltpu.CompilerParams(vmem_limit_bytes=50 * 1024 * 1024),
        cost_estimate=pl.CostEstimate(
            flops=2 * 9 * CELLS * D * D, bytes_accessed=12_000_000, transcendentals=0
        ),
        name="finish",
    )(req, slots, acc, shifts, grads)


def ring(value, by):
    length = lax.axis_size("tile")
    return lax.ppermute(value, "tile", [(i, (i + by) % length) for i in range(length)])


def turned(row, flag):
    return jnp.where(flag == 1, row[::-1], row)


def exchange(value, axes="tile"):
    return lax.all_to_all(value, axes, split_axis=0, concat_axis=0, tiled=True)


def local(
    grid,
    tokens,
    targets,
    sub_masks,
    live_counts,
    edge_turns,
    w_query,
    w_key,
    w_value,
    w_out,
    w_conv,
    token_cotan,
):
    ntile = lax.axis_size("tile")
    ndev = ntile * lax.axis_size("win")
    me = lax.axis_index("tile")
    turns = edge_turns[0]
    nblocks = tokens.shape[1] // BT
    i32 = jnp.int32

    dest = targets[0, :, 0]
    order = jnp.arange(nblocks, dtype=i32)
    earlier = order[None, :] < order[:, None]
    rank = jnp.sum((earlier & (dest[None, :] == dest[:, None])).astype(i32), axis=1)
    chunk = (rank + dest + me) % 2
    sub = jnp.sum(sub_masks[0] * jnp.arange(SUB, dtype=i32)[None, :], axis=1)
    tiles = jnp.arange(ntile, dtype=i32)
    chunks = jnp.arange(2, dtype=i32)
    at_slot = (dest[:, None, None] == tiles[None, :, None]) & (
        chunk[:, None, None] == chunks[None, None, :]
    )
    want = SUB + jnp.sum(jnp.where(at_slot, sub[:, None, None] - SUB, 0), axis=0)
    req = exchange(want)

    place = jnp.sum((earlier & (chunk[None, :] == chunk[:, None])).astype(i32), axis=1)
    sizes = jnp.sum((chunk[:, None] == chunks[None, :]).astype(i32), axis=0)
    step = jnp.minimum(order[None, :], sizes[:, None] - 1)
    picked = (
        (place[None, None, :] == step[:, :, None]) & (chunk[None, None, :] == chunks[:, None, None])
    ).astype(i32)
    live = live_counts[0]
    columns = jnp.stack([order, dest, live], axis=0)
    lists = jnp.sum(picked[:, None] * columns[None, :, None, :], axis=-1)
    meta = jnp.concatenate(
        [lists, jnp.broadcast_to(sizes[:, None, None], (2, 1, nblocks))], axis=1
    )

    field = grid[0]
    above = turned(ring(field[-1], 1), turns[0])
    below = turned(ring(field[0], -1), turns[1])
    rimmed = jnp.concatenate([above[None], field, below[None]], axis=0).reshape(-1, D)
    send_a, send_b, shifts = hidden_sends(req, rimmed, w_conv.reshape(9, D, D))

    wkv = jnp.concatenate([w_key, w_value], axis=1)
    weights = (w_query, w_query.T, wkv, wkv.T, w_out, w_out.T)
    x = tokens[0].reshape(nblocks, BT, D)
    cot = token_cotan[0].reshape(nblocks, BT, D)
    got_a = exchange(send_a)
    got_b = exchange(send_b)
    zeros = jnp.zeros((4 * D, D), f32)
    out_a, tgrad_a, back_a, grads_a = attend(meta[0], got_a, x, cot, weights, zeros, ())
    ret_a = exchange(back_a)
    token_out, token_grad, back_b, grads = attend(
        meta[1], got_b, x, cot, weights, grads_a, (out_a, tgrad_a)
    )
    ret_b = exchange(back_b)
    acc = gather_slots(req, ret_a)
    hidden_grad, sums = finish(req, ret_b, acc, shifts, grads)

    parts = exchange(sums, ("tile", "win")).reshape(ndev, -1, D)
    share = jnp.sum(parts.astype(f32), axis=0).astype(bf16)
    spread = jnp.broadcast_to(share[None], (ndev,) + share.shape).reshape(-1, D)
    total = exchange(spread, ("tile", "win")).astype(f32).reshape(13, D, D)

    hidden_back = hidden_grad.astype(bf16).reshape(RY, RX, D)
    padded = jnp.pad(hidden_back, ((0, 0), (1, 1), (0, 0)))
    taps = []
    for a in range(3):
        piece = jnp.zeros((RY, RX, D), f32)
        for b in range(3):
            cells = padded[:, 2 - b : 2 - b + RX].reshape(-1, D)
            piece = piece + mm_nt(cells, w_conv[a, b]).reshape(RY, RX, D)
        taps.append(piece)
    from_below = ring(turned(taps[0][0], turns[0]), -1)
    from_above = ring(turned(taps[2][-1], turns[1]), 1)
    field_grad = hidden_grad.reshape(RY, RX, D) + taps[1]
    field_grad = field_grad + jnp.concatenate([taps[0][1:], from_below[None]], axis=0)
    field_grad = field_grad + jnp.concatenate([from_above[None], taps[2][:-1]], axis=0)
    grid_grad = field_grad.astype(bf16)[None]

    def scaled(grad):
        return grad / jnp.sqrt(jnp.mean(grad * grad) + EPSILON)

    upd_query = scaled(total[0]).T
    upd_key = scaled(total[1]).T
    upd_value = scaled(total[2]).T
    upd_out = scaled(total[3])
    upd_conv = scaled(total[4:]).transpose(0, 2, 1).reshape(3, 3, D, D)
    return (
        token_out.reshape(1, -1, D),
        token_grad.reshape(1, -1, D),
        grid_grad,
        upd_query,
        upd_key,
        upd_value,
        upd_out,
        upd_conv,
    )


def solution(mesh):
    return jax.shard_map(
        local,
        mesh=mesh,
        in_specs=(
            P("win", "tile", None, None),
            P("win", "tile", None),
            P("win", "tile", None),
            P("win", "tile", None),
            P("win", "tile"),
            P("tile", None),
            P(),
            P(),
            P(),
            P(),
            P(),
            P("win", "tile", None),
        ),
        out_specs=(
            P("win", "tile", None),
            P("win", "tile", None),
            P("win", "tile", None, None),
            P(),
            P(),
            P(),
            P(),
            P(),
        ),
        check_vma=False,
    )
```

```python
import math

import jax
import jax.numpy as jnp
from jax import lax
from jax.experimental import pallas as pl
from jax.experimental.pallas import tpu as pltpu
from jax.sharding import PartitionSpec as P

D = 256
HEADS = 8
HD = 32
BT = 128
RY = 32
RX = 32
SUB = 8
KEYS = 128
CELLS = RY * RX
EPSILON = 1e-06
SCALE = 1.0 / math.sqrt(HD)
EXP2_SCALE = SCALE * math.log2(math.e)
STEP = 8
AHEAD = 2

f32 = jnp.float32
bf16 = jnp.bfloat16


def mm(a, b):
    return lax.dot_general(a, b, (((1,), (0,)), ((), ())), preferred_element_type=f32)


def mm_nt(a, b):
    return lax.dot_general(a, b, (((1,), (1,)), ((), ())), preferred_element_type=f32)


def whole(shape):
    return pl.BlockSpec(shape, lambda *_: (0,) * len(shape))


def hidden_kernel(req_ref, rim_ref, w_ref, send_a, send_b, shifts_ref, hid, sems):
    rim = rim_ref[...].astype(f32)
    rows = rim.shape[0]
    col = lax.broadcasted_iota(jnp.int32, (rows, D), 0) % RX
    shifts_ref[0] = jnp.where(col == 0, 0.0, pltpu.roll(rim, 1, 0)).astype(bf16)
    shifts_ref[1] = rim_ref[...]
    shifts_ref[2] = jnp.where(col == RX - 1, 0.0, pltpu.roll(rim, rows - 1, 0)).astype(bf16)
    piece = CELLS // 4

    @pl.loop(0, 4)
    def _(i):
        base = i * piece
        total = rim_ref[pl.ds(pl.multiple_of(base + RX, RX), piece), :].astype(f32)
        for a in range(3):
            for b in range(3):
                cells = shifts_ref[b, pl.ds(pl.multiple_of(base + a * RX, RX), piece), :]
                total = total + mm(cells, w_ref[3 * a + b])
        hid[pl.ds(pl.multiple_of(base, piece), piece), :] = total.astype(bf16)

    count = send_a.shape[0]

    def copy(c, out, s):
        sub = jnp.minimum(req_ref[s, c], SUB - 1)
        source = hid.at[pl.ds(pl.multiple_of(sub * KEYS, KEYS), KEYS), :]
        return pltpu.make_async_copy(source, out.at[s], sems.at[c])

    @pl.loop(0, count)
    def _(s):
        copy(0, send_a, s).start()
        copy(1, send_b, s).start()

    @pl.loop(0, count)
    def _(s):
        copy(0, send_a, s).wait()
        copy(1, send_b, s).wait()


def hidden_sends(req, rimmed, w_conv):
    count = req.shape[0]
    slots = jax.ShapeDtypeStruct((count, KEYS, D), bf16)
    rows = (RY + 2) * RX
    return pl.pallas_call(
        hidden_kernel,
        out_shape=(slots, slots, jax.ShapeDtypeStruct((3, rows, D), bf16)),
        in_specs=[
            pl.BlockSpec(memory_space=pltpu.SMEM),
            pl.BlockSpec(memory_space=pltpu.VMEM),
            pl.BlockSpec(memory_space=pltpu.VMEM),
        ],
        out_specs=(
            pl.BlockSpec(memory_space=pltpu.HBM),
            pl.BlockSpec(memory_space=pltpu.HBM),
            pl.BlockSpec(memory_space=pltpu.VMEM),
        ),
        scratch_shapes=[
            pltpu.VMEM((CELLS, D), bf16),
            pltpu.SemaphoreType.DMA((2,)),
        ],
        compiler_params=pltpu.CompilerParams(vmem_limit_bytes=60 * 1024 * 1024),
        cost_estimate=pl.CostEstimate(
            flops=2 * 9 * CELLS * D * D, bytes_accessed=20_000_000, transcendentals=0
        ),
        name="conv_sends",
    )(req, rimmed, w_conv)


def attend_kernel(meta, wq, wq_t, wkv, wkv_t, wo, wo_t, grads_in, slots, xs, cots, *rest):
    outs, tgrads, hgrads, grads_ref, hbuf, xbuf, cbuf, obuf, tbuf, gbuf, in_sems, out_sems = rest[-12:]
    count = meta[3, 0]
    steps = (count + 1) // 2

    def loads(i, slot):
        copies = []
        for u in range(2):
            k = jnp.minimum(2 * i + u, count - 1)
            block, tile = meta[0, k], meta[1, k]
            rows = pl.ds(u * BT, BT)
            copies += [
                pltpu.make_async_copy(slots.at[tile], hbuf.at[slot, rows], in_sems.at[slot, 3 * u]),
                pltpu.make_async_copy(xs.at[block], xbuf.at[slot, rows], in_sems.at[slot, 3 * u + 1]),
                pltpu.make_async_copy(cots.at[block], cbuf.at[slot, rows], in_sems.at[slot, 3 * u + 2]),
            ]
        return copies

    def stores(i, slot, u):
        k = jnp.minimum(2 * i + u, count - 1)
        block, tile = meta[0, k], meta[1, k]
        rows = pl.ds(u * BT, BT)
        return [
            pltpu.make_async_copy(gbuf.at[slot, u], hgrads.at[tile], out_sems.at[slot, 3 * u]),
            pltpu.make_async_copy(obuf.at[slot, rows], outs.at[block], out_sems.at[slot, 3 * u + 1]),
            pltpu.make_async_copy(tbuf.at[slot, rows], tgrads.at[block], out_sems.at[slot, 3 * u + 2]),
        ]

    def start_stores(i, slot):
        for c in stores(i, slot, 0):
            c.start()

        @pl.when(2 * i + 1 < count)
        def _():
            for c in stores(i, slot, 1):
                c.start()

    def wait_stores(i, slot):
        for c in stores(i, slot, 0):
            c.wait()

        @pl.when(2 * i + 1 < count)
        def _():
            for c in stores(i, slot, 1):
                c.wait()

    for c in loads(0, 0):
        c.start()
    grads_ref[...] = grads_in[...]
    zero = jnp.zeros((HD, BT), bf16)
    none = jnp.zeros((2 * HD, 2 * BT), bf16)

    def paired(t, p):
        first = t[2 * HD * p : 2 * HD * p + HD]
        second = t[2 * HD * p + HD : 2 * HD * p + 2 * HD]
        return jnp.concatenate(
            [
                jnp.concatenate([first, zero], axis=1),
                jnp.concatenate([zero, second], axis=1),
            ],
            axis=0,
        )

    def deep(pair, p):
        return jnp.concatenate([pair, none] if p % 2 == 0 else [none, pair], axis=0)

    @pl.loop(0, steps)
    def _(i):
        slot = lax.rem(i, 2)

        @pl.when(i + 1 < steps)
        def _():
            for c in loads(i + 1, 1 - slot):
                c.start()

        for c in loads(i, slot):
            c.wait()

        @pl.when(i >= 2)
        def _():
            wait_stores(i - 2, slot)

        live0 = meta[2, 2 * i]
        live1 = jnp.where(2 * i + 1 < count, meta[2, jnp.minimum(2 * i + 1, count - 1)], 0)
        h = hbuf[slot]
        x = xbuf[slot]
        row = lax.broadcasted_iota(jnp.int32, (2 * BT, D), 0)
        lane = lax.broadcasted_iota(jnp.int32, (D, 2 * BT), 1)
        row_live = row < jnp.where(row < BT, live0, live1 + BT)
        lane_live = lane < jnp.where(lane < BT, live0, live1 + BT)
        cot = jnp.where(row_live, cbuf[slot].astype(f32), 0.0).astype(bf16)
        kv = mm(h, wkv[...]).astype(bf16)
        kv_t = mm_nt(wkv_t[...], h).astype(bf16)
        q_t = mm_nt(wq_t[...], x).astype(bf16)
        d_t = mm_nt(wo[...], cot).astype(bf16)
        att_rows, qg_rows, kg_rows, vg_rows = [[], []], [[], []], [[], []], [[], []]
        def first(p, u):
            rows = slice(u * BT, u * BT + BT)
            half = 128 * (p // 2)
            q2 = paired(q_t[:, rows], p)
            d2 = paired(d_t[:, rows], p)
            scores = mm(kv[rows, half : half + 128], deep(q2, p))
            wg = mm(kv[rows, D + half : D + half + 128], deep(d2, p))
            return q2, d2, scores, wg

        def second(q2, d2, scores, wg):
            top = jnp.max(scores, axis=0, keepdims=True)
            e = jnp.exp2((scores - top) * EXP2_SCALE)
            wf = e * (1.0 / jnp.sum(e, axis=0, keepdims=True))
            mean = jnp.sum(wf * wg, axis=0, keepdims=True)
            sg = (wf * (wg - mean)).astype(bf16)
            return q2, d2, wf.astype(bf16), sg

        def third(p, u, q2, d2, w, sg):
            rows = slice(u * BT, u * BT + BT)
            feats = slice(2 * HD * p, 2 * HD * p + 2 * HD)
            v_feats = slice(D + 2 * HD * p, D + 2 * HD * p + 2 * HD)
            att = mm(kv_t[v_feats, rows], w)
            att_rows[u] += [att[:HD, :BT], att[HD:, BT:]]
            qg = mm(kv_t[feats, rows], sg)
            qg_rows[u] += [qg[:HD, :BT], qg[HD:, BT:]]
            kg_rows[u].append(mm_nt(q2, sg) * SCALE)
            vg_rows[u].append(mm_nt(d2, w))

        units = [(p, u) for p in range(HEADS // 2) for u in range(2)]
        ready, soft = {}, {}
        for k in range(len(units) + AHEAD + 1):
            if k < len(units):
                ready[k] = first(*units[k])
            j = k - AHEAD
            if 0 <= j < len(units):
                soft[j] = second(*ready.pop(j))
            if 0 <= j - 1 < len(units):
                third(*units[j - 1], *soft.pop(j - 1))

        def joined(rows):
            return jnp.concatenate([jnp.concatenate(r, axis=0) for r in rows], axis=1)

        att_t = joined(att_rows).astype(bf16)
        qg_t = (joined(qg_rows) * SCALE).astype(bf16)
        kvg_t = joined([kg_rows[u] + vg_rows[u] for u in range(2)]).astype(bf16)
        mixed = jnp.where(lane_live, mm(wo_t[...], att_t), 0.0)
        obuf[slot] = mixed.T.astype(bf16)
        tbuf[slot] = mm(wq[...], qg_t).T.astype(bf16)
        back = mm(wkv[...], kvg_t).astype(bf16)
        gbuf[slot, 0] = back[:, :BT]
        gbuf[slot, 1] = back[:, BT:]
        grads_ref[0:256] += mm(qg_t, x)
        grads_ref[256:768] += mm(kvg_t, h)
        grads_ref[768:1024] += mm(att_t, cot)
        start_stores(i, slot)

    @pl.when(steps >= 2)
    def _():
        wait_stores(steps - 2, lax.rem(steps, 2))

    wait_stores(steps - 1, lax.rem(steps - 1, 2))


def attend(meta, slots, x, cot, weights, grads, kept):
    nblocks = x.shape[0]
    count = slots.shape[0]
    vmem = pl.BlockSpec(memory_space=pltpu.VMEM)
    remote = pl.BlockSpec(memory_space=pltpu.HBM)
    args = [meta, *weights, grads, slots, x, cot, *kept]
    first_kept = len(args) - len(kept)
    token_shape = jax.ShapeDtypeStruct((nblocks, BT, D), bf16)
    pair = pltpu.VMEM((2, 2 * BT, D), bf16)
    return pl.pallas_call(
        attend_kernel,
        out_shape=(
            token_shape,
            token_shape,
            jax.ShapeDtypeStruct((count, D, KEYS), bf16),
            jax.ShapeDtypeStruct((4 * D, D), f32),
        ),
        in_specs=[pl.BlockSpec(memory_space=pltpu.SMEM)]
        + [vmem] * (len(weights) + 1)
        + [remote] * (3 + len(kept)),
        out_specs=(remote, remote, remote, vmem),
        scratch_shapes=[pair] * 5
        + [
            pltpu.VMEM((2, 2, D, KEYS), bf16),
            pltpu.SemaphoreType.DMA((2, 6)),
            pltpu.SemaphoreType.DMA((2, 6)),
        ],
        input_output_aliases={first_kept + j: j for j in range(len(kept))},
        compiler_params=pltpu.CompilerParams(vmem_limit_bytes=60 * 1024 * 1024),
        cost_estimate=pl.CostEstimate(
            flops=nblocks * 400_000_000, bytes_accessed=nblocks * 400_000, transcendentals=0
        ),
        name="attend",
    )(*args)


def add_slots(req_ref, slots_ref, acc_ref, column):
    i = pl.program_id(0)
    for j in range(STEP):
        sub = req_ref[i * STEP + j, column]

        @pl.when(sub < SUB)
        def _():
            at = pl.ds(pl.multiple_of(sub * D, D), D)
            acc_ref[at, :] += slots_ref[j].astype(f32)


def gather_kernel(req_ref, slots_ref, acc_ref):
    @pl.when(pl.program_id(0) == 0)
    def _():
        acc_ref[...] = jnp.zeros_like(acc_ref)

    add_slots(req_ref, slots_ref, acc_ref, 0)


def finish_kernel(req_ref, slots_ref, acc_in, shifts_ref, grads_ref, hgrad_ref, sums_ref, acc_ref, back_t):
    i = pl.program_id(0)

    @pl.when(i == 0)
    def _():
        acc_ref[...] = acc_in[...]

    add_slots(req_ref, slots_ref, acc_ref, 1)

    @pl.when(i == pl.num_programs(0) - 1)
    def _():
        sums_ref[0 : 4 * D] = grads_ref[...].astype(bf16)
        if sums_ref.shape[0] > 13 * D:
            sums_ref[13 * D :] = jnp.zeros((sums_ref.shape[0] - 13 * D, D), bf16)
        for s in range(SUB):
            part = acc_ref[s * D : (s + 1) * D, :]
            hgrad_ref[s * KEYS : (s + 1) * KEYS, :] = part.T
            back_t[:, s * KEYS : (s + 1) * KEYS] = part.astype(bf16)
        for a in range(3):
            for b in range(3):
                at = (4 + 3 * a + b) * D
                cells = shifts_ref[b, a * RX : a * RX + CELLS, :]
                sums_ref[at : at + D] = mm(back_t[...], cells).astype(bf16)


def slot_specs(count):
    return [
        pl.BlockSpec(memory_space=pltpu.SMEM),
        pl.BlockSpec((STEP, D, KEYS), lambda i: (i, 0, 0)),
    ]


def gather_slots(req, slots):
    count = slots.shape[0]
    return pl.pallas_call(
        gather_kernel,
        out_shape=jax.ShapeDtypeStruct((SUB * D, KEYS), f32),
        grid=(count // STEP,),
        in_specs=slot_specs(count),
        out_specs=whole((SUB * D, KEYS)),
        compiler_params=pltpu.CompilerParams(vmem_limit_bytes=60 * 1024 * 1024),
        cost_estimate=pl.CostEstimate(
            flops=count * D * KEYS, bytes_accessed=count * D * KEYS * 2, transcendentals=0
        ),
        name="gather_slots",
    )(req, slots)


def finish(req, slots, acc, shifts, grads, rows):
    count = slots.shape[0]
    return pl.pallas_call(
        finish_kernel,
        out_shape=(
            jax.ShapeDtypeStruct((CELLS, D), f32),
            jax.ShapeDtypeStruct((rows, D), bf16),
        ),
        grid=(count // STEP,),
        in_specs=slot_specs(count)
        + [whole(acc.shape), whole(shifts.shape), whole(grads.shape)],
        out_specs=(whole((CELLS, D)), whole((rows, D))),
        scratch_shapes=[
            pltpu.VMEM((SUB * D, KEYS), f32),
            pltpu.VMEM((D, CELLS), bf16),
        ],
        compiler_params=pltpu.CompilerParams(vmem_limit_bytes=60 * 1024 * 1024),
        cost_estimate=pl.CostEstimate(
            flops=2 * 9 * CELLS * D * D, bytes_accessed=12_000_000, transcendentals=0
        ),
        name="finish",
    )(req, slots, acc, shifts, grads)


def normalize_kernel(sums_ref, query_ref, key_ref, value_ref, out_ref, conv_ref):
    def part(k):
        return sums_ref[k * D : (k + 1) * D, :].astype(f32)

    def squares(k):
        item = part(k)
        return jnp.sum(jnp.sum(item * item, axis=0, keepdims=True), axis=1, keepdims=True)

    def factor(total, size):
        return 1.0 / jnp.sqrt(total / size + EPSILON)

    for k, ref in enumerate((query_ref, key_ref, value_ref)):
        ref[...] = (part(k) * factor(squares(k), D * D)).T
    out_ref[...] = part(3) * factor(squares(3), D * D)
    total = squares(4)
    for k in range(5, 13):
        total = total + squares(k)
    scale = factor(total, 9 * D * D)
    for k in range(9):
        conv_ref[k] = (part(4 + k) * scale).T


def normalize(sums):
    square = jax.ShapeDtypeStruct((D, D), f32)
    return pl.pallas_call(
        normalize_kernel,
        out_shape=(square,) * 4 + (jax.ShapeDtypeStruct((9, D, D), f32),),
        in_specs=[pl.BlockSpec(memory_space=pltpu.VMEM)],
        out_specs=(pl.BlockSpec(memory_space=pltpu.VMEM),) * 5,
        compiler_params=pltpu.CompilerParams(vmem_limit_bytes=60 * 1024 * 1024),
        cost_estimate=pl.CostEstimate(flops=4_000_000, bytes_accessed=6_000_000, transcendentals=0),
        name="normalize",
    )(sums)


def ring(value, by):
    length = lax.axis_size("tile")
    return lax.ppermute(value, "tile", [(i, (i + by) % length) for i in range(length)])


def turned(row, flag):
    return jnp.where(flag == 1, row[::-1], row)


def exchange(value, axes="tile"):
    return lax.all_to_all(value, axes, split_axis=0, concat_axis=0, tiled=True)


def local(
    grid,
    tokens,
    targets,
    sub_masks,
    live_counts,
    edge_turns,
    w_query,
    w_key,
    w_value,
    w_out,
    w_conv,
    token_cotan,
):
    ntile = lax.axis_size("tile")
    ndev = ntile * lax.axis_size("win")
    me = lax.axis_index("tile")
    turns = edge_turns[0]
    nblocks = tokens.shape[1] // BT
    i32 = jnp.int32

    dest = targets[0, :, 0]
    order = jnp.arange(nblocks, dtype=i32)
    earlier = order[None, :] < order[:, None]
    rank = jnp.sum((earlier & (dest[None, :] == dest[:, None])).astype(i32), axis=1)
    chunk = (rank + dest + me) % 2
    sub = jnp.sum(sub_masks[0] * jnp.arange(SUB, dtype=i32)[None, :], axis=1)
    tiles = jnp.arange(ntile, dtype=i32)
    chunks = jnp.arange(2, dtype=i32)
    at_slot = (dest[:, None, None] == tiles[None, :, None]) & (
        chunk[:, None, None] == chunks[None, None, :]
    )
    want = SUB + jnp.sum(jnp.where(at_slot, sub[:, None, None] - SUB, 0), axis=0)
    req = exchange(want)

    place = jnp.sum((earlier & (chunk[None, :] == chunk[:, None])).astype(i32), axis=1)
    sizes = jnp.sum((chunk[:, None] == chunks[None, :]).astype(i32), axis=0)
    step = jnp.minimum(order[None, :], sizes[:, None] - 1)
    picked = (
        (place[None, None, :] == step[:, :, None]) & (chunk[None, None, :] == chunks[:, None, None])
    ).astype(i32)
    live = live_counts[0]
    columns = jnp.stack([order, dest, live], axis=0)
    lists = jnp.sum(picked[:, None] * columns[None, :, None, :], axis=-1)
    meta = jnp.concatenate(
        [lists, jnp.broadcast_to(sizes[:, None, None], (2, 1, nblocks))], axis=1
    )

    field = grid[0]
    above = turned(ring(field[-1], 1), turns[0])
    below = turned(ring(field[0], -1), turns[1])
    rimmed = jnp.concatenate([above[None], field, below[None]], axis=0).reshape(-1, D)
    send_a, send_b, shifts = hidden_sends(req, rimmed, w_conv.reshape(9, D, D))

    wkv = jnp.concatenate([w_key, w_value], axis=1)
    weights = (w_query, w_query.T, wkv, wkv.T, w_out, w_out.T)
    x = tokens[0].reshape(nblocks, BT, D)
    cot = token_cotan[0].reshape(nblocks, BT, D)
    got_a = exchange(send_a)
    got_b = exchange(send_b)
    zeros = jnp.zeros((4 * D, D), f32)
    out_a, tgrad_a, back_a, grads_a = attend(meta[0], got_a, x, cot, weights, zeros, ())
    ret_a = exchange(back_a)
    token_out, token_grad, back_b, grads = attend(
        meta[1], got_b, x, cot, weights, grads_a, (out_a, tgrad_a)
    )
    ret_b = exchange(back_b)
    acc = gather_slots(req, ret_a)
    each = -(-13 * D // (16 * ndev)) * 16
    hidden_grad, sums = finish(req, ret_b, acc, shifts, grads, ndev * each)

    parts = exchange(sums, ("tile", "win")).reshape(ndev, -1, D)
    share = jnp.sum(parts.astype(f32), axis=0).astype(bf16)
    spread = jnp.broadcast_to(share[None], (ndev,) + share.shape).reshape(-1, D)
    updates = normalize(exchange(spread, ("tile", "win")))

    hidden_back = hidden_grad.astype(bf16).reshape(RY, RX, D)
    padded = jnp.pad(hidden_back, ((0, 0), (1, 1), (0, 0)))
    taps = []
    for a in range(3):
        piece = jnp.zeros((RY, RX, D), f32)
        for b in range(3):
            cells = padded[:, 2 - b : 2 - b + RX].reshape(-1, D)
            piece = piece + mm_nt(cells, w_conv[a, b]).reshape(RY, RX, D)
        taps.append(piece)
    from_below = ring(turned(taps[0][0], turns[0]), -1)
    from_above = ring(turned(taps[2][-1], turns[1]), 1)
    field_grad = hidden_grad.reshape(RY, RX, D) + taps[1]
    field_grad = field_grad + jnp.concatenate([taps[0][1:], from_below[None]], axis=0)
    field_grad = field_grad + jnp.concatenate([from_above[None], taps[2][:-1]], axis=0)
    grid_grad = field_grad.astype(bf16)[None]

    return (
        token_out.reshape(1, -1, D),
        token_grad.reshape(1, -1, D),
        grid_grad,
        *updates[:4],
        updates[4].reshape(3, 3, D, D),
    )


def solution(mesh):
    return jax.shard_map(
        local,
        mesh=mesh,
        in_specs=(
            P("win", "tile", None, None),
            P("win", "tile", None),
            P("win", "tile", None),
            P("win", "tile", None),
            P("win", "tile"),
            P("tile", None),
            P(),
            P(),
            P(),
            P(),
            P(),
            P("win", "tile", None),
        ),
        out_specs=(
            P("win", "tile", None),
            P("win", "tile", None),
            P("win", "tile", None, None),
            P(),
            P(),
            P(),
            P(),
            P(),
        ),
        check_vma=False,
    )
```

```python
import functools
import math

import jax
import jax.numpy as jnp
from jax import lax
from jax.experimental import pallas as pl
from jax.experimental.pallas import tpu as pltpu
from jax.sharding import PartitionSpec as P

D = 256
HEADS = 8
HD = 32
BT = 128
RY = 32
RX = 32
SUB = 8
KEYS = 128
CELLS = RY * RX
EPSILON = 1e-06
SCALE = 1.0 / math.sqrt(HD)
EXP2_SCALE = SCALE * math.log2(math.e)
AHEAD = 2

f32 = jnp.float32
bf16 = jnp.bfloat16


def mm(a, b):
    return lax.dot_general(a, b, (((1,), (0,)), ((), ())), preferred_element_type=f32)


def mm_nt(a, b):
    return lax.dot_general(a, b, (((1,), (1,)), ((), ())), preferred_element_type=f32)


VMEM = pl.BlockSpec(memory_space=pltpu.VMEM)
HBM = pl.BlockSpec(memory_space=pltpu.HBM)
PARAMS = pltpu.CompilerParams(vmem_limit_bytes=60 * 1024 * 1024)


def hidden_kernel(rim_ref, w_ref, send_ref, shifts_ref):
    rim = rim_ref[...].astype(f32)
    rows = rim.shape[0]
    col = lax.broadcasted_iota(jnp.int32, (rows, D), 0) % RX
    shifts_ref[0] = jnp.where(col == 0, 0.0, pltpu.roll(rim, 1, 0)).astype(bf16)
    shifts_ref[1] = rim_ref[...]
    shifts_ref[2] = jnp.where(col == RX - 1, 0.0, pltpu.roll(rim, rows - 1, 0)).astype(bf16)
    slices = send_ref.shape[1]
    piece = CELLS // 4

    @pl.loop(0, 4)
    def _(i):
        base = i * piece
        total = rim_ref[pl.ds(pl.multiple_of(base + RX, RX), piece), :].astype(f32)
        for a in range(3):
            for b in range(3):
                cells = shifts_ref[b, pl.ds(pl.multiple_of(base + a * RX, RX), piece), :]
                total = total + mm(cells, w_ref[3 * a + b])
        hidden = total.astype(bf16)
        for k in range(piece // KEYS):
            cuts = range(k * KEYS, (k + 1) * KEYS, slices)
            send_ref[i * (piece // KEYS) + k] = jnp.concatenate(
                [hidden[at : at + slices] for at in cuts], axis=1
            )


def hidden_slices(rimmed, w_conv, slices):
    rows = (RY + 2) * RX
    return pl.pallas_call(
        hidden_kernel,
        out_shape=(
            jax.ShapeDtypeStruct((SUB, slices, KEYS * D // slices), bf16),
            jax.ShapeDtypeStruct((3, rows, D), bf16),
        ),
        in_specs=[VMEM, VMEM],
        out_specs=(VMEM, VMEM),
        compiler_params=PARAMS,
        cost_estimate=pl.CostEstimate(
            flops=2 * 9 * CELLS * D * D, bytes_accessed=6_000_000, transcendentals=0
        ),
        name="conv_slices",
    )(rimmed, w_conv)


def pick_kernel(table_ref, ids_ref, out_ref):
    names = table_ref.shape[0]
    blocks, sources = ids_ref.shape
    group = 256 // blocks
    lane = lax.broadcasted_iota(jnp.int32, (blocks, names), 1)
    for g in range(0, sources, group):
        hot = [
            jnp.where(lane == ids_ref[:, g + k : g + k + 1], 1.0, 0.0).astype(bf16)
            for k in range(group)
        ]
        rows = mm(jnp.concatenate(hot, axis=0), table_ref[...]).astype(bf16)
        for k in range(group):
            out_ref[g + k] = rows[k * blocks : (k + 1) * blocks]


def pick(table, ids):
    blocks, sources = ids.shape
    width = table.shape[1]
    return pl.pallas_call(
        pick_kernel,
        out_shape=jax.ShapeDtypeStruct((sources, blocks, width), bf16),
        in_specs=[VMEM, VMEM],
        out_specs=VMEM,
        compiler_params=PARAMS,
        cost_estimate=pl.CostEstimate(
            flops=2 * sources * blocks * table.size, bytes_accessed=4_000_000, transcendentals=0
        ),
        name="pick",
    )(table, ids)


def gather_kernel(ids_ref, slots_ref, *rest):
    acc_ref, out_ref = rest[:-1], rest[-1]
    names = out_ref.shape[0]
    rows = slots_ref.shape[0]
    piece = min(512, rows)
    total = acc_ref[0][...] if acc_ref else None
    name = lax.broadcasted_iota(jnp.int32, (names, piece), 0)
    for at in range(0, rows, piece):
        hot = jnp.where(name == ids_ref[:, at : at + piece], 1.0, 0.0).astype(bf16)
        part = mm(hot, slots_ref[at : at + piece, :])
        total = part if total is None else total + part
    out_ref[...] = total.astype(out_ref.dtype)


def gather(ids, slots, names, acc, dtype):
    width = slots.shape[1]
    return pl.pallas_call(
        gather_kernel,
        out_shape=jax.ShapeDtypeStruct((names, width), dtype),
        in_specs=[VMEM] * (2 + len(acc)),
        out_specs=VMEM,
        compiler_params=PARAMS,
        cost_estimate=pl.CostEstimate(
            flops=2 * slots.size * names, bytes_accessed=4_000_000, transcendentals=0
        ),
        name="gather",
    )(ids, slots, *acc)


def attend_kernel(base, live, wq, wq_t, wkv, wkv_t, wo, wo_t, grads_in, slots, xs, cots, *rest):
    outs, tgrads, hgrads, grads_ref, hbuf, xbuf, cbuf, obuf, tbuf, gbuf, in_sems, out_sems = rest[-12:]
    steps = slots.shape[0] // 2
    slices = slots.shape[1]

    def loads(i, slot):
        blocks = pl.ds(base + 2 * i, 2)
        return [
            pltpu.make_async_copy(slots.at[pl.ds(2 * i, 2)], hbuf.at[slot], in_sems.at[slot, 0]),
            pltpu.make_async_copy(xs.at[blocks], xbuf.at[slot], in_sems.at[slot, 1]),
            pltpu.make_async_copy(cots.at[blocks], cbuf.at[slot], in_sems.at[slot, 2]),
        ]

    def stores(i, slot):
        blocks = pl.ds(base + 2 * i, 2)
        return [
            pltpu.make_async_copy(gbuf.at[slot], hgrads.at[pl.ds(2 * i, 2)], out_sems.at[slot, 0]),
            pltpu.make_async_copy(obuf.at[slot], outs.at[blocks], out_sems.at[slot, 1]),
            pltpu.make_async_copy(tbuf.at[slot], tgrads.at[blocks], out_sems.at[slot, 2]),
        ]

    for c in loads(0, 0):
        c.start()
    grads_ref[...] = grads_in[...]
    zero = jnp.zeros((HD, BT), bf16)
    none = jnp.zeros((2 * HD, 2 * BT), bf16)

    def paired(t, p):
        first = t[2 * HD * p : 2 * HD * p + HD]
        second = t[2 * HD * p + HD : 2 * HD * p + 2 * HD]
        return jnp.concatenate(
            [
                jnp.concatenate([first, zero], axis=1),
                jnp.concatenate([zero, second], axis=1),
            ],
            axis=0,
        )

    def deep(pair, p):
        return jnp.concatenate([pair, none] if p % 2 == 0 else [none, pair], axis=0)

    @pl.loop(0, steps)
    def _(i):
        slot = lax.rem(i, 2)

        @pl.when(i + 1 < steps)
        def _():
            for c in loads(i + 1, 1 - slot):
                c.start()

        for c in loads(i, slot):
            c.wait()

        @pl.when(i >= 2)
        def _():
            for c in stores(i - 2, slot):
                c.wait()

        live0 = live[0, base + 2 * i]
        live1 = live[0, base + 2 * i + 1]
        sliced = hbuf[slot]
        h = jnp.concatenate(
            [sliced[u, :, at : at + D] for u in range(2) for at in range(0, sliced.shape[2], D)],
            axis=0,
        )
        x = xbuf[slot].reshape(2 * BT, D)
        row = lax.broadcasted_iota(jnp.int32, (2 * BT, D), 0)
        lane = lax.broadcasted_iota(jnp.int32, (D, 2 * BT), 1)
        row_live = row < jnp.where(row < BT, live0, live1 + BT)
        lane_live = lane < jnp.where(lane < BT, live0, live1 + BT)
        cot = jnp.where(row_live, cbuf[slot].reshape(2 * BT, D).astype(f32), 0.0).astype(bf16)
        kv = mm(h, wkv[...]).astype(bf16)
        kv_t = mm_nt(wkv_t[...], h).astype(bf16)
        q_t = mm_nt(wq_t[...], x).astype(bf16)
        d_t = mm_nt(wo[...], cot).astype(bf16)
        att_rows, qg_rows, kg_rows, vg_rows = [[], []], [[], []], [[], []], [[], []]
        def first(p, u):
            rows = slice(u * BT, u * BT + BT)
            half = 128 * (p // 2)
            q2 = paired(q_t[:, rows], p)
            d2 = paired(d_t[:, rows], p)
            scores = mm(kv[rows, half : half + 128], deep(q2, p))
            wg = mm(kv[rows, D + half : D + half + 128], deep(d2, p))
            return q2, d2, scores, wg

        def second(q2, d2, scores, wg):
            top = jnp.max(scores, axis=0, keepdims=True)
            e = jnp.exp2((scores - top) * EXP2_SCALE)
            wf = e * (1.0 / jnp.sum(e, axis=0, keepdims=True))
            mean = jnp.sum(wf * wg, axis=0, keepdims=True)
            sg = (wf * (wg - mean)).astype(bf16)
            return q2, d2, wf.astype(bf16), sg

        def third(p, u, q2, d2, w, sg):
            rows = slice(u * BT, u * BT + BT)
            feats = slice(2 * HD * p, 2 * HD * p + 2 * HD)
            v_feats = slice(D + 2 * HD * p, D + 2 * HD * p + 2 * HD)
            att = mm(kv_t[v_feats, rows], w)
            att_rows[u] += [att[:HD, :BT], att[HD:, BT:]]
            qg = mm(kv_t[feats, rows], sg)
            qg_rows[u] += [qg[:HD, :BT], qg[HD:, BT:]]
            kg_rows[u].append(mm_nt(q2, sg) * SCALE)
            vg_rows[u].append(mm_nt(d2, w))

        units = [(p, u) for p in range(HEADS // 2) for u in range(2)]
        ready, soft = {}, {}
        for k in range(len(units) + AHEAD + 1):
            if k < len(units):
                ready[k] = first(*units[k])
            j = k - AHEAD
            if 0 <= j < len(units):
                soft[j] = second(*ready.pop(j))
            if 0 <= j - 1 < len(units):
                third(*units[j - 1], *soft.pop(j - 1))

        def joined(rows):
            return jnp.concatenate([jnp.concatenate(r, axis=0) for r in rows], axis=1)

        att_t = joined(att_rows).astype(bf16)
        qg_t = (joined(qg_rows) * SCALE).astype(bf16)
        kvg_t = joined([kg_rows[u] + vg_rows[u] for u in range(2)]).astype(bf16)
        mixed = jnp.where(lane_live, mm(wo_t[...], att_t), 0.0)
        obuf[slot] = mixed.T.astype(bf16).reshape(2, BT, D)
        tbuf[slot] = mm(wq[...], qg_t).T.astype(bf16).reshape(2, BT, D)
        back = mm(wkv[...], kvg_t).astype(bf16)
        for u in range(2):
            gbuf[slot, u] = jnp.concatenate(
                [back[at : at + slices, u * BT : u * BT + BT] for at in range(0, D, slices)], axis=1
            )
        grads_ref[0:256] += mm(qg_t, x)
        grads_ref[256:768] += mm(kvg_t, h)
        grads_ref[768:1024] += mm(att_t, cot)
        for c in stores(i, slot):
            c.start()

    for i in range(max(0, steps - 2), steps):
        for c in stores(i, i % 2):
            c.wait()


def attend(base, live, slots, x, cot, weights, grads, kept):
    args = [live, *weights, grads, slots, x, cot, *kept]
    first_kept = len(args) - len(kept)
    token_shape = jax.ShapeDtypeStruct(x.shape, bf16)
    sliced = pltpu.VMEM((2, 2) + slots.shape[1:], bf16)
    pair = pltpu.VMEM((2, 2, BT, D), bf16)
    return pl.pallas_call(
        functools.partial(attend_kernel, base),
        out_shape=(
            token_shape,
            token_shape,
            jax.ShapeDtypeStruct(slots.shape, bf16),
            jax.ShapeDtypeStruct((4 * D, D), f32),
        ),
        in_specs=[pl.BlockSpec(memory_space=pltpu.SMEM)]
        + [VMEM] * (len(weights) + 1)
        + [HBM] * (3 + len(kept)),
        out_specs=(HBM, HBM, HBM, VMEM),
        scratch_shapes=[
            sliced,
            pair,
            pair,
            pair,
            pair,
            sliced,
            pltpu.SemaphoreType.DMA((2, 3)),
            pltpu.SemaphoreType.DMA((2, 3)),
        ],
        input_output_aliases={first_kept + j: j for j in range(len(kept))},
        compiler_params=PARAMS,
        cost_estimate=pl.CostEstimate(
            flops=slots.shape[0] * 800_000_000,
            bytes_accessed=slots.shape[0] * 800_000,
            transcendentals=0,
        ),
        name="attend",
    )(*args)


def finish_kernel(slices_ref, shifts_ref, grads_ref, hgrad_ref, sums_ref, back_t):
    slices = slices_ref.shape[1]
    sums_ref[0 : 4 * D] = grads_ref[...].astype(bf16)
    if sums_ref.shape[0] > 13 * D:
        sums_ref[13 * D :] = jnp.zeros((sums_ref.shape[0] - 13 * D, D), bf16)
    for s in range(SUB):
        cells = slice(s * KEYS, (s + 1) * KEYS)
        part = jnp.concatenate(
            [slices_ref[s, :, at : at + KEYS] for at in range(0, D * KEYS // slices, KEYS)], axis=0
        )
        back_t[:, cells] = part
        hgrad_ref[cells, :] = part.astype(f32).T.astype(bf16)
    for a in range(3):
        for b in range(3):
            at = (4 + 3 * a + b) * D
            sums_ref[at : at + D] = mm(
                back_t[...], shifts_ref[b, a * RX : a * RX + CELLS, :]
            ).astype(bf16)


def finish(slices, shifts, grads, rows):
    return pl.pallas_call(
        finish_kernel,
        out_shape=(
            jax.ShapeDtypeStruct((CELLS, D), bf16),
            jax.ShapeDtypeStruct((rows, D), bf16),
        ),
        in_specs=[VMEM] * 3,
        out_specs=(VMEM, VMEM),
        scratch_shapes=[pltpu.VMEM((D, CELLS), bf16)],
        compiler_params=PARAMS,
        cost_estimate=pl.CostEstimate(
            flops=2 * 9 * CELLS * D * D, bytes_accessed=6_000_000, transcendentals=0
        ),
        name="finish",
    )(slices, shifts, grads)


def normalize_kernel(sums_ref, query_ref, key_ref, value_ref, out_ref, conv_ref):
    def part(k):
        return sums_ref[k * D : (k + 1) * D, :].astype(f32)

    def squares(k):
        item = part(k)
        return jnp.sum(jnp.sum(item * item, axis=0, keepdims=True), axis=1, keepdims=True)

    def factor(total, size):
        return 1.0 / jnp.sqrt(total / size + EPSILON)

    for k, ref in enumerate((query_ref, key_ref, value_ref)):
        ref[...] = (part(k) * factor(squares(k), D * D)).T
    out_ref[...] = part(3) * factor(squares(3), D * D)
    total = squares(4)
    for k in range(5, 13):
        total = total + squares(k)
    scale = factor(total, 9 * D * D)
    for k in range(9):
        conv_ref[k] = (part(4 + k) * scale).T


def normalize(sums):
    square = jax.ShapeDtypeStruct((D, D), f32)
    return pl.pallas_call(
        normalize_kernel,
        out_shape=(square,) * 4 + (jax.ShapeDtypeStruct((9, D, D), f32),),
        in_specs=[pl.BlockSpec(memory_space=pltpu.VMEM)],
        out_specs=(pl.BlockSpec(memory_space=pltpu.VMEM),) * 5,
        compiler_params=pltpu.CompilerParams(vmem_limit_bytes=60 * 1024 * 1024),
        cost_estimate=pl.CostEstimate(flops=4_000_000, bytes_accessed=6_000_000, transcendentals=0),
        name="normalize",
    )(sums)


def ring(value, by):
    length = lax.axis_size("tile")
    return lax.ppermute(value, "tile", [(i, (i + by) % length) for i in range(length)])


def turned(row, flag):
    return jnp.where(flag == 1, row[::-1], row)


def exchange(value, axes="tile"):
    return lax.all_to_all(value, axes, split_axis=0, concat_axis=0, tiled=True)


def local(
    grid,
    tokens,
    targets,
    sub_masks,
    live_counts,
    edge_turns,
    w_query,
    w_key,
    w_value,
    w_out,
    w_conv,
    token_cotan,
):
    ntile = lax.axis_size("tile")
    ndev = ntile * lax.axis_size("win")
    turns = edge_turns[0]
    nblocks = tokens.shape[1] // BT

    sub = jnp.sum(sub_masks[0] * jnp.arange(SUB, dtype=jnp.int32)[None, :], axis=1)
    own = targets[0, :, 0] * SUB + sub
    ids = exchange(jnp.broadcast_to(own[None, :], (ntile, nblocks)))

    field = grid[0]
    above = turned(ring(field[-1], 1), turns[0])
    below = turned(ring(field[0], -1), turns[1])
    rimmed = jnp.concatenate([above[None], field, below[None]], axis=0).reshape(-1, D)
    sliced, shifts = hidden_slices(rimmed, w_conv.reshape(9, D, D), ntile)
    table = exchange(sliced.transpose(1, 0, 2)).reshape(ntile * SUB, -1)

    wkv = jnp.concatenate([w_key, w_value], axis=1)
    weights = (w_query, w_query.T, wkv, wkv.T, w_out, w_out.T)
    x = tokens[0].reshape(nblocks, BT, D)
    cot = token_cotan[0].reshape(nblocks, BT, D)
    half = nblocks // 2
    grads = jnp.zeros((4 * D, D), f32)
    got = [exchange(pick(table, ids[:, c * half : (c + 1) * half].T)) for c in range(2)]
    kept, returned = (), []
    for c in range(2):
        token_out, token_grad, back, grads = attend(
            c * half, live_counts, got[c].transpose(1, 0, 2), x, cot, weights, grads, kept
        )
        kept = (token_out, token_grad)
        returned.append(exchange(back.transpose(1, 0, 2)).reshape(ntile * half, -1))
    rows = [ids[:, c * half : (c + 1) * half].reshape(1, -1) for c in range(2)]
    acc = gather(rows[0], returned[0], ntile * SUB, (), f32)
    home = gather(rows[1], returned[1], ntile * SUB, (acc,), bf16)
    home = exchange(home.reshape(ntile, SUB, -1)).transpose(1, 0, 2)
    each = -(-13 * D // (16 * ndev)) * 16
    hidden_back, sums = finish(home, shifts, grads, ndev * each)

    parts = exchange(sums, ("tile", "win")).reshape(ndev, -1, D)
    share = jnp.sum(parts.astype(f32), axis=0).astype(bf16)
    spread = jnp.broadcast_to(share[None], (ndev,) + share.shape).reshape(-1, D)
    updates = normalize(exchange(spread, ("tile", "win")))

    hidden_back = hidden_back.reshape(RY, RX, D)
    padded = jnp.pad(hidden_back, ((0, 0), (1, 1), (0, 0)))
    taps = []
    for a in range(3):
        piece = jnp.zeros((RY, RX, D), f32)
        for b in range(3):
            cells = padded[:, 2 - b : 2 - b + RX].reshape(-1, D)
            piece = piece + mm_nt(cells, w_conv[a, b]).reshape(RY, RX, D)
        taps.append(piece)
    from_below = ring(turned(taps[0][0], turns[0]), -1)
    from_above = ring(turned(taps[2][-1], turns[1]), 1)
    field_grad = hidden_back.astype(f32) + taps[1]
    field_grad = field_grad + jnp.concatenate([taps[0][1:], from_below[None]], axis=0)
    field_grad = field_grad + jnp.concatenate([from_above[None], taps[2][:-1]], axis=0)
    grid_grad = field_grad.astype(bf16)[None]

    return (
        token_out.reshape(1, -1, D),
        token_grad.reshape(1, -1, D),
        grid_grad,
        *updates[:4],
        updates[4].reshape(3, 3, D, D),
    )


def solution(mesh):
    return jax.shard_map(
        local,
        mesh=mesh,
        in_specs=(
            P("win", "tile", None, None),
            P("win", "tile", None),
            P("win", "tile", None),
            P("win", "tile", None),
            P("win", "tile"),
            P("tile", None),
            P(),
            P(),
            P(),
            P(),
            P(),
            P("win", "tile", None),
        ),
        out_specs=(
            P("win", "tile", None),
            P("win", "tile", None),
            P("win", "tile", None, None),
            P(),
            P(),
            P(),
            P(),
            P(),
        ),
        check_vma=False,
    )
```

```python
import functools
import math

import jax
import jax.numpy as jnp
from jax import lax
from jax.experimental import pallas as pl
from jax.experimental.pallas import tpu as pltpu
from jax.sharding import PartitionSpec as P

D = 256
HEADS = 8
HD = 32
BT = 128
RY = 32
RX = 32
SUB = 8
LANES = 128
KEYS = 128
CELLS = RY * RX
EPSILON = 1e-06
SCALE = 1.0 / math.sqrt(HD)
EXP2_SCALE = SCALE * math.log2(math.e)
AHEAD = 3

f32 = jnp.float32
bf16 = jnp.bfloat16


def mm(a, b):
    return lax.dot_general(a, b, (((1,), (0,)), ((), ())), preferred_element_type=f32)


def mm_nt(a, b):
    return lax.dot_general(a, b, (((1,), (1,)), ((), ())), preferred_element_type=f32)


VMEM = pl.BlockSpec(memory_space=pltpu.VMEM)
HBM = pl.BlockSpec(memory_space=pltpu.HBM)
PARAMS = pltpu.CompilerParams(vmem_limit_bytes=60 * 1024 * 1024)


def hidden_kernel(rim_ref, w_ref, send_ref, shifts_ref):
    rim = rim_ref[...].astype(f32)
    rows = rim.shape[0]
    col = lax.broadcasted_iota(jnp.int32, (rows, D), 0) % RX
    shifts_ref[0] = jnp.where(col == 0, 0.0, pltpu.roll(rim, 1, 0)).astype(bf16)
    shifts_ref[1] = rim_ref[...]
    shifts_ref[2] = jnp.where(col == RX - 1, 0.0, pltpu.roll(rim, rows - 1, 0)).astype(bf16)
    slices = send_ref.shape[1]
    piece = CELLS // 4

    @pl.loop(0, 4)
    def _(i):
        base = i * piece
        total = rim_ref[pl.ds(pl.multiple_of(base + RX, RX), piece), :].astype(f32)
        for a in range(3):
            for b in range(3):
                cells = shifts_ref[b, pl.ds(pl.multiple_of(base + a * RX, RX), piece), :]
                total = total + mm(cells, w_ref[3 * a + b])
        hidden = total.astype(bf16)
        for k in range(piece // KEYS):
            cuts = range(k * KEYS, (k + 1) * KEYS, slices)
            send_ref[i * (piece // KEYS) + k] = jnp.concatenate(
                [hidden[at : at + slices] for at in cuts], axis=1
            )


def hidden_slices(rimmed, w_conv, slices):
    rows = (RY + 2) * RX
    return pl.pallas_call(
        hidden_kernel,
        out_shape=(
            jax.ShapeDtypeStruct((SUB, slices, KEYS * D // slices), bf16),
            jax.ShapeDtypeStruct((3, rows, D), bf16),
        ),
        in_specs=[VMEM, VMEM],
        out_specs=(VMEM, VMEM),
        compiler_params=PARAMS,
        cost_estimate=pl.CostEstimate(
            flops=2 * 9 * CELLS * D * D, bytes_accessed=6_000_000, transcendentals=0
        ),
        name="conv_slices",
    )(rimmed, w_conv)


def pick_kernel(table_ref, ids_ref, out_ref):
    names = table_ref.shape[0]
    width = out_ref.shape[2]
    blocks, sources = ids_ref.shape
    group = 256 // blocks
    lane = lax.broadcasted_iota(jnp.int32, (blocks, names), 1)
    for g in range(0, sources, group):
        hot = [
            jnp.where(lane == ids_ref[:, g + k : g + k + 1], 1.0, 0.0).astype(bf16)
            for k in range(group)
        ]
        rows = mm(jnp.concatenate(hot, axis=0), table_ref[:, :width]).astype(bf16)
        for k in range(group):
            out_ref[g + k] = rows[k * blocks : (k + 1) * blocks]


def pick(table, ids, width):
    blocks, sources = ids.shape
    return pl.pallas_call(
        pick_kernel,
        out_shape=jax.ShapeDtypeStruct((sources, blocks, width), bf16),
        in_specs=[VMEM, VMEM],
        out_specs=VMEM,
        compiler_params=PARAMS,
        cost_estimate=pl.CostEstimate(
            flops=2 * sources * blocks * table.size, bytes_accessed=4_000_000, transcendentals=0
        ),
        name="pick",
    )(table, ids)


def gather_kernel(ids_ref, slots_ref, *rest):
    acc_ref, out_ref = rest[:-1], rest[-1]
    names = out_ref.shape[0]
    rows = slots_ref.shape[0]
    piece = min(512, rows)
    total = acc_ref[0][...] if acc_ref else None
    name = lax.broadcasted_iota(jnp.int32, (names, piece), 0)
    for at in range(0, rows, piece):
        hot = jnp.where(name == ids_ref[:, at : at + piece], 1.0, 0.0).astype(bf16)
        part = mm(hot, slots_ref[at : at + piece, :])
        total = part if total is None else total + part
    out_ref[...] = total.astype(out_ref.dtype)


def gather(ids, slots, names, acc, dtype):
    width = slots.shape[1]
    return pl.pallas_call(
        gather_kernel,
        out_shape=jax.ShapeDtypeStruct((names, width), dtype),
        in_specs=[VMEM] * (2 + len(acc)),
        out_specs=VMEM,
        compiler_params=PARAMS,
        cost_estimate=pl.CostEstimate(
            flops=2 * slots.size * names, bytes_accessed=4_000_000, transcendentals=0
        ),
        name="gather",
    )(ids, slots, *acc)


def attend_kernel(base, live, wq, wq_t, wkv, wkv_t, wo, wo_t, grads_in, slots, xs, cots, *rest):
    outs, tgrads, hgrads, grads_ref = rest[-19:-15]
    hbuf, xbuf, cbuf, obuf, tbuf, gbuf = rest[-15:-9]
    kvs, kvts, qts, dts, att_s, qg_s, kvg_s, in_sems, out_sems = rest[-9:]
    steps = slots.shape[0] // 2
    slices = slots.shape[1]

    def loads(i):
        blocks = pl.ds(base + 2 * i, 2)
        slot = lax.rem(i, 4)
        return [
            pltpu.make_async_copy(slots.at[pl.ds(2 * i, 2)], hbuf.at[slot], in_sems.at[slot, 0]),
            pltpu.make_async_copy(xs.at[blocks], xbuf.at[slot], in_sems.at[slot, 1]),
            pltpu.make_async_copy(cots.at[blocks], cbuf.at[slot], in_sems.at[slot, 2]),
        ]

    def stores(i):
        blocks = pl.ds(base + 2 * i, 2)
        slot = lax.rem(i, 2)
        return [
            pltpu.make_async_copy(gbuf.at[slot], hgrads.at[pl.ds(2 * i, 2)], out_sems.at[slot, 0]),
            pltpu.make_async_copy(obuf.at[slot], outs.at[blocks], out_sems.at[slot, 1]),
            pltpu.make_async_copy(tbuf.at[slot], tgrads.at[blocks], out_sems.at[slot, 2]),
        ]

    zero = jnp.zeros((HD, BT), bf16)

    def paired(t, p):
        top = t[2 * HD * p : 2 * HD * p + HD]
        low = t[2 * HD * p + HD : 2 * HD * p + 2 * HD]
        return jnp.concatenate(
            [jnp.concatenate([top, zero], axis=1), jnp.concatenate([zero, low], axis=1)], axis=0
        )

    def lives(i):
        at = base + 2 * jnp.minimum(i, steps - 1)
        return live[0, at], live[0, at + 1]

    def cells(i):
        sliced = hbuf[lax.rem(i, 4)]
        return jnp.concatenate(
            [sliced[u, :, at : at + D] for u in range(2) for at in range(0, sliced.shape[2], D)],
            axis=0,
        )

    def rows_of(buf, i):
        return buf[lax.rem(i, 4)].reshape(2 * BT, D)

    def head(i):
        slot = lax.rem(i, 2)

        def keys():
            kvs[slot] = mm(cells(i), wkv[...]).astype(bf16)

        def keys_t():
            kvts[slot] = mm_nt(wkv_t[...], cells(i)).astype(bf16)

        def queries():
            qts[slot] = mm_nt(wq_t[...], rows_of(xbuf, i)).astype(bf16)

        def cotangents():
            live0, live1 = lives(i)
            row = lax.broadcasted_iota(jnp.int32, (2 * BT, D), 0)
            row_live = row < jnp.where(row < BT, live0, live1 + BT)
            cot = jnp.where(row_live, rows_of(cbuf, i).astype(f32), 0.0).astype(bf16)
            cbuf[lax.rem(i, 4)] = cot.reshape(2, BT, D)
            dts[slot] = mm_nt(wo[...], cot).astype(bf16)

        return [cotangents, queries, keys, keys_t]

    def tail(i):
        slot = lax.rem(i + 2, 2)

        def mixed():
            live0, live1 = lives(i)
            lane = lax.broadcasted_iota(jnp.int32, (D, 2 * BT), 1)
            lane_live = lane < jnp.where(lane < BT, live0, live1 + BT)
            out = jnp.where(lane_live, mm(wo_t[...], att_s[...]), 0.0)
            obuf[slot] = out.T.astype(bf16).reshape(2, BT, D)

        def token_grad():
            tbuf[slot] = mm(wq[...], qg_s[...]).T.astype(bf16).reshape(2, BT, D)

        def hidden_grad():
            back = mm(wkv[...], kvg_s[...]).astype(bf16)
            for u in range(2):
                gbuf[slot, u] = jnp.concatenate(
                    [back[at : at + slices, u * BT : u * BT + BT] for at in range(0, D, slices)],
                    axis=1,
                )

        def weight_grads():
            grads_ref[0:256] += mm(qg_s[...], rows_of(xbuf, i + 4))
            grads_ref[256:768] += mm(kvg_s[...], cells(i + 4))
            grads_ref[768:1024] += mm(att_s[...], rows_of(cbuf, i + 4))

        return [hidden_grad, mixed, token_grad, weight_grads]

    def attention(i, between):
        slot = lax.rem(i, 2)
        kv, kv_t, q_t, d_t = kvs[slot], kvts[slot], qts[slot], dts[slot]
        att_rows, qg_rows, kg_rows, vg_rows = [[], []], [[], []], [[], []], [[], []]

        def first(p, u):
            rows = slice(u * BT, u * BT + BT)
            at = 2 * HD * p
            q2 = paired(q_t[:, rows], p)
            d2 = paired(d_t[:, rows], p)
            scores = mm(kv[rows, at : at + 2 * HD], q2)
            wg = mm(kv[rows, D + at : D + at + 2 * HD], d2)
            return q2, d2, scores, wg

        def second(q2, d2, scores, wg):
            top = jnp.max(scores, axis=0, keepdims=True)
            e = jnp.exp2((scores - top) * EXP2_SCALE)
            wf = e * (1.0 / jnp.sum(e, axis=0, keepdims=True))
            mean = jnp.sum(wf * wg, axis=0, keepdims=True)
            sg = (wf * (wg - mean)).astype(bf16)
            return q2, d2, wf.astype(bf16), sg

        def third(p, u, q2, d2, w, sg):
            rows = slice(u * BT, u * BT + BT)
            feats = slice(2 * HD * p, 2 * HD * p + 2 * HD)
            v_feats = slice(D + 2 * HD * p, D + 2 * HD * p + 2 * HD)
            att = mm(kv_t[v_feats, rows], w)
            att_rows[u] += [att[:HD, :BT], att[HD:, BT:]]
            qg = mm(kv_t[feats, rows], sg)
            qg_rows[u] += [qg[:HD, :BT], qg[HD:, BT:]]
            kg_rows[u].append(mm_nt(q2, sg) * SCALE)
            vg_rows[u].append(mm_nt(d2, w))

        units = [(p, u) for p in range(HEADS // 2) for u in range(2)]
        ready, soft = {}, {}
        between = list(between)
        for k in range(len(units) + AHEAD + 1):
            if k < len(units):
                ready[k] = first(*units[k])
            if between and k >= 1:
                between.pop(0)()
            j = k - AHEAD
            if 0 <= j < len(units):
                soft[j] = second(*ready.pop(j))
            if 0 <= j - 1 < len(units):
                third(*units[j - 1], *soft.pop(j - 1))
        for piece in between:
            piece()

        def joined(rows):
            return jnp.concatenate([jnp.concatenate(r, axis=0) for r in rows], axis=1)

        att_s[...] = joined(att_rows).astype(bf16)
        qg_s[...] = (joined(qg_rows) * SCALE).astype(bf16)
        kvg_s[...] = joined([kg_rows[u] + vg_rows[u] for u in range(2)]).astype(bf16)

    for c in loads(0):
        c.start()
    for c in loads(1):
        c.start()
    grads_ref[...] = grads_in[...]
    for ref in (att_s, qg_s, kvg_s):
        ref[...] = jnp.zeros_like(ref)
    for ref in (hbuf, xbuf, cbuf):
        ref[3] = jnp.zeros(ref.shape[1:], bf16)
    for c in loads(0):
        c.wait()
    for piece in head(0):
        piece()

    @pl.loop(0, steps)
    def _(i):
        @pl.when(i + 2 < steps)
        def _():
            for c in loads(i + 2):
                c.start()

        @pl.when(i + 1 < steps)
        def _():
            for c in loads(i + 1):
                c.wait()

        @pl.when(i >= 3)
        def _():
            for c in stores(i - 3):
                c.wait()

        attention(i, [piece for two in zip(tail(i - 1), head(i + 1)) for piece in two])

        @pl.when(i >= 1)
        def _():
            for c in stores(i - 1):
                c.start()

    for c in stores(steps - 3):
        c.wait()
    for piece in tail(steps - 1):
        piece()
    for c in stores(steps - 1):
        c.start()
    for i in (steps - 2, steps - 1):
        for c in stores(i):
            c.wait()


def attend(base, live, slots, x, cot, weights, grads, kept):
    args = [live, *weights, grads, slots, x, cot, *kept]
    first_kept = len(args) - len(kept)
    token_shape = jax.ShapeDtypeStruct(x.shape, bf16)
    return pl.pallas_call(
        functools.partial(attend_kernel, base),
        out_shape=(
            token_shape,
            token_shape,
            jax.ShapeDtypeStruct(slots.shape, bf16),
            jax.ShapeDtypeStruct((4 * D, D), f32),
        ),
        in_specs=[pl.BlockSpec(memory_space=pltpu.SMEM)]
        + [VMEM] * (len(weights) + 1)
        + [HBM] * (3 + len(kept)),
        out_specs=(HBM, HBM, HBM, VMEM),
        scratch_shapes=[
            pltpu.VMEM((4, 2) + slots.shape[1:], bf16),
            pltpu.VMEM((4, 2, BT, D), bf16),
            pltpu.VMEM((4, 2, BT, D), bf16),
            pltpu.VMEM((2, 2, BT, D), bf16),
            pltpu.VMEM((2, 2, BT, D), bf16),
            pltpu.VMEM((2, 2) + slots.shape[1:], bf16),
            pltpu.VMEM((2, 2 * KEYS, 2 * D), bf16),
            pltpu.VMEM((2, 2 * D, 2 * KEYS), bf16),
            pltpu.VMEM((2, D, 2 * BT), bf16),
            pltpu.VMEM((2, D, 2 * BT), bf16),
            pltpu.VMEM((D, 2 * BT), bf16),
            pltpu.VMEM((D, 2 * BT), bf16),
            pltpu.VMEM((2 * D, 2 * KEYS), bf16),
            pltpu.SemaphoreType.DMA((4, 3)),
            pltpu.SemaphoreType.DMA((2, 3)),
        ],
        input_output_aliases={first_kept + j: j for j in range(len(kept))},
        compiler_params=PARAMS,
        cost_estimate=pl.CostEstimate(
            flops=slots.shape[0] * 800_000_000,
            bytes_accessed=slots.shape[0] * 800_000,
            transcendentals=0,
        ),
        name="attend",
    )(*args)


def finish_kernel(slices_ref, shifts_ref, grads_ref, hgrad_ref, sums_ref, back_t):
    slices = slices_ref.shape[1]
    used = 13 * D * D // LANES

    def put(k, grad):
        for j, at in enumerate(range(0, D, LANES)):
            row = (k * (D // LANES) + j) * D
            sums_ref[row : row + D] = grad[:, at : at + LANES].astype(bf16)

    for k in range(4):
        put(k, grads_ref[k * D : (k + 1) * D])
    if sums_ref.shape[0] > used:
        sums_ref[used:] = jnp.zeros((sums_ref.shape[0] - used, LANES), bf16)
    for s in range(SUB):
        cells = slice(s * KEYS, (s + 1) * KEYS)
        part = jnp.concatenate(
            [slices_ref[s, :, at : at + KEYS] for at in range(0, D * KEYS // slices, KEYS)], axis=0
        )
        back_t[:, cells] = part
        hgrad_ref[cells, :] = part.astype(f32).T.astype(bf16)
    for a in range(3):
        for b in range(3):
            put(4 + 3 * a + b, mm(back_t[...], shifts_ref[b, a * RX : a * RX + CELLS, :]))


def finish(slices, shifts, grads, rows):
    return pl.pallas_call(
        finish_kernel,
        out_shape=(
            jax.ShapeDtypeStruct((CELLS, D), bf16),
            jax.ShapeDtypeStruct((rows, LANES), bf16),
        ),
        in_specs=[VMEM] * 3,
        out_specs=(VMEM, VMEM),
        scratch_shapes=[pltpu.VMEM((D, CELLS), bf16)],
        compiler_params=PARAMS,
        cost_estimate=pl.CostEstimate(
            flops=2 * 9 * CELLS * D * D, bytes_accessed=6_000_000, transcendentals=0
        ),
        name="finish",
    )(slices, shifts, grads)


def normalize_kernel(sums_ref, query_ref, key_ref, value_ref, out_ref, conv_ref):
    def part(k):
        rows = [(k * (D // LANES) + j) * D for j in range(D // LANES)]
        return jnp.concatenate([sums_ref[r : r + D].astype(f32) for r in rows], axis=1)

    def squares(k):
        item = part(k)
        return jnp.sum(jnp.sum(item * item, axis=0, keepdims=True), axis=1, keepdims=True)

    def factor(total, size):
        return 1.0 / jnp.sqrt(total / size + EPSILON)

    for k, ref in enumerate((query_ref, key_ref, value_ref)):
        ref[...] = (part(k) * factor(squares(k), D * D)).T
    out_ref[...] = part(3) * factor(squares(3), D * D)
    total = squares(4)
    for k in range(5, 13):
        total = total + squares(k)
    scale = factor(total, 9 * D * D)
    for k in range(9):
        conv_ref[k] = (part(4 + k) * scale).T


def normalize(sums):
    square = jax.ShapeDtypeStruct((D, D), f32)
    return pl.pallas_call(
        normalize_kernel,
        out_shape=(square,) * 4 + (jax.ShapeDtypeStruct((9, D, D), f32),),
        in_specs=[pl.BlockSpec(memory_space=pltpu.VMEM)],
        out_specs=(pl.BlockSpec(memory_space=pltpu.VMEM),) * 5,
        compiler_params=pltpu.CompilerParams(vmem_limit_bytes=60 * 1024 * 1024),
        cost_estimate=pl.CostEstimate(flops=4_000_000, bytes_accessed=6_000_000, transcendentals=0),
        name="normalize",
    )(sums)


def ring(value, by):
    length = lax.axis_size("tile")
    return lax.ppermute(value, "tile", [(i, (i + by) % length) for i in range(length)])


def turned(row, flag):
    return jnp.where(flag == 1, row[::-1], row)


def exchange(value, axes="tile"):
    return lax.all_to_all(value, axes, split_axis=0, concat_axis=0, tiled=True)


def local(
    grid,
    tokens,
    targets,
    sub_masks,
    live_counts,
    edge_turns,
    w_query,
    w_key,
    w_value,
    w_out,
    w_conv,
    token_cotan,
):
    ntile = lax.axis_size("tile")
    ndev = ntile * lax.axis_size("win")
    turns = edge_turns[0]
    nblocks = tokens.shape[1] // BT

    sub = jnp.sum(sub_masks[0] * jnp.arange(SUB, dtype=jnp.int32)[None, :], axis=1)
    names = jnp.concatenate([targets[0, :, 0], sub]).astype(bf16)
    names = jnp.pad(names[None], ((0, SUB - 1), (0, 0)))

    field = grid[0]
    above = turned(ring(field[-1], 1), turns[0])
    below = turned(ring(field[0], -1), turns[1])
    rimmed = jnp.concatenate([above[None], field, below[None]], axis=0).reshape(-1, D)
    sliced, shifts = hidden_slices(rimmed, w_conv.reshape(9, D, D), ntile)
    width = sliced.shape[2]
    sliced = jnp.concatenate(
        [sliced.transpose(1, 0, 2), jnp.broadcast_to(names[None], (ntile,) + names.shape)], axis=2
    )
    table = exchange(sliced)
    ids = table[:, 0, width:].astype(jnp.int32)
    ids = ids[:, :nblocks] * SUB + ids[:, nblocks:]
    table = table.reshape(ntile * SUB, -1)

    wkv = jnp.concatenate([w_key, w_value], axis=1)
    weights = (w_query, w_query.T, wkv, wkv.T, w_out, w_out.T)
    x = tokens[0].reshape(nblocks, BT, D)
    cot = token_cotan[0].reshape(nblocks, BT, D)
    half = nblocks // 2
    grads = jnp.zeros((4 * D, D), f32)
    got = [exchange(pick(table, ids[:, c * half : (c + 1) * half].T, width)) for c in range(2)]
    kept, returned = (), []
    for c in range(2):
        token_out, token_grad, back, grads = attend(
            c * half, live_counts, got[c].transpose(1, 0, 2), x, cot, weights, grads, kept
        )
        kept = (token_out, token_grad)
        returned.append(exchange(back.transpose(1, 0, 2)).reshape(ntile * half, -1))
    rows = [ids[:, c * half : (c + 1) * half].reshape(1, -1) for c in range(2)]
    acc = gather(rows[0], returned[0], ntile * SUB, (), f32)
    home = gather(rows[1], returned[1], ntile * SUB, (acc,), bf16)
    home = exchange(home.reshape(ntile, SUB, -1)).transpose(1, 0, 2)
    each = -(-13 * D * D // LANES // (8 * ndev)) * 8
    hidden_back, sums = finish(home, shifts, grads, ndev * each)

    parts = exchange(sums.reshape(ndev, -1, LANES), ("tile", "win"))
    share = jnp.sum(parts.astype(f32), axis=0).astype(bf16)

    hidden_back = hidden_back.reshape(RY, RX, D)
    padded = jnp.pad(hidden_back, ((0, 0), (1, 1), (0, 0)))
    taps = []
    for a in range(3):
        piece = jnp.zeros((RY, RX, D), f32)
        for b in range(3):
            cells = padded[:, 2 - b : 2 - b + RX].reshape(-1, D)
            piece = piece + mm_nt(cells, w_conv[a, b]).reshape(RY, RX, D)
        taps.append(piece)
    from_below = ring(turned(taps[0][0], turns[0]), -1)
    from_above = ring(turned(taps[2][-1], turns[1]), 1)
    field_grad = hidden_back.astype(f32) + taps[1]
    field_grad = field_grad + jnp.concatenate([taps[0][1:], from_below[None]], axis=0)
    field_grad = field_grad + jnp.concatenate([from_above[None], taps[2][:-1]], axis=0)
    grid_grad = field_grad.astype(bf16)[None]
    share, grid_grad = lax.optimization_barrier((share, grid_grad))
    spread = jnp.broadcast_to(share[None], (ndev,) + share.shape)
    updates = normalize(exchange(spread, ("tile", "win")).reshape(-1, LANES))

    return (
        token_out.reshape(1, -1, D),
        token_grad.reshape(1, -1, D),
        grid_grad,
        *updates[:4],
        updates[4].reshape(3, 3, D, D),
    )


def solution(mesh):
    return jax.shard_map(
        local,
        mesh=mesh,
        in_specs=(
            P("win", "tile", None, None),
            P("win", "tile", None),
            P("win", "tile", None),
            P("win", "tile", None),
            P("win", "tile"),
            P("tile", None),
            P(),
            P(),
            P(),
            P(),
            P(),
            P("win", "tile", None),
        ),
        out_specs=(
            P("win", "tile", None),
            P("win", "tile", None),
            P("win", "tile", None, None),
            P(),
            P(),
            P(),
            P(),
            P(),
        ),
        check_vma=False,
    )
```

```python
import functools
import math

import jax
import jax.numpy as jnp
from jax import lax
from jax.experimental import pallas as pl
from jax.experimental.pallas import tpu as pltpu
from jax.sharding import PartitionSpec as P

D = 256
HEADS = 8
HD = 32
BT = 128
RY = 32
RX = 32
SUB = 8
LANES = 128
KEYS = 128
CELLS = RY * RX
EPSILON = 1e-06
SCALE = 1.0 / math.sqrt(HD)
EXP2_SCALE = SCALE * math.log2(math.e)
AHEAD = 3
PAIRS = 2

f32 = jnp.float32
bf16 = jnp.bfloat16


def mm(a, b):
    return lax.dot_general(a, b, (((1,), (0,)), ((), ())), preferred_element_type=f32)


def mm_nt(a, b):
    return lax.dot_general(a, b, (((1,), (1,)), ((), ())), preferred_element_type=f32)


VMEM = pl.BlockSpec(memory_space=pltpu.VMEM)
HBM = pl.BlockSpec(memory_space=pltpu.HBM)
PARAMS = pltpu.CompilerParams(vmem_limit_bytes=60 * 1024 * 1024)


def hidden_kernel(rim_ref, w_ref, send_ref, shifts_ref):
    rim = rim_ref[...].astype(f32)
    rows = rim.shape[0]
    col = lax.broadcasted_iota(jnp.int32, (rows, D), 0) % RX
    shifts_ref[0] = jnp.where(col == 0, 0.0, pltpu.roll(rim, 1, 0)).astype(bf16)
    shifts_ref[1] = rim_ref[...]
    shifts_ref[2] = jnp.where(col == RX - 1, 0.0, pltpu.roll(rim, rows - 1, 0)).astype(bf16)
    slices = send_ref.shape[1]
    piece = CELLS // 4

    @pl.loop(0, 4)
    def _(i):
        base = i * piece
        total = rim_ref[pl.ds(pl.multiple_of(base + RX, RX), piece), :].astype(f32)
        for a in range(3):
            for b in range(3):
                cells = shifts_ref[b, pl.ds(pl.multiple_of(base + a * RX, RX), piece), :]
                total = total + mm(cells, w_ref[3 * a + b])
        hidden = total.astype(bf16)
        for k in range(piece // KEYS):
            cuts = range(k * KEYS, (k + 1) * KEYS, slices)
            send_ref[i * (piece // KEYS) + k] = jnp.concatenate(
                [hidden[at : at + slices] for at in cuts], axis=1
            )


def hidden_slices(rimmed, w_conv, slices):
    rows = (RY + 2) * RX
    return pl.pallas_call(
        hidden_kernel,
        out_shape=(
            jax.ShapeDtypeStruct((SUB, slices, KEYS * D // slices), bf16),
            jax.ShapeDtypeStruct((3, rows, D), bf16),
        ),
        in_specs=[VMEM, VMEM],
        out_specs=(VMEM, VMEM),
        compiler_params=PARAMS,
        cost_estimate=pl.CostEstimate(
            flops=2 * 9 * CELLS * D * D, bytes_accessed=6_000_000, transcendentals=0
        ),
        name="conv_slices",
    )(rimmed, w_conv)


def pick_kernel(table_ref, ids_ref, out_ref):
    names = table_ref.shape[0]
    width = out_ref.shape[2]
    blocks, sources = ids_ref.shape
    group = 256 // blocks
    lane = lax.broadcasted_iota(jnp.int32, (blocks, names), 1)
    for g in range(0, sources, group):
        hot = [
            jnp.where(lane == ids_ref[:, g + k : g + k + 1], 1.0, 0.0).astype(bf16)
            for k in range(group)
        ]
        rows = mm(jnp.concatenate(hot, axis=0), table_ref[:, :width]).astype(bf16)
        for k in range(group):
            out_ref[g + k] = rows[k * blocks : (k + 1) * blocks]


def pick(table, ids, width):
    blocks, sources = ids.shape
    return pl.pallas_call(
        pick_kernel,
        out_shape=jax.ShapeDtypeStruct((sources, blocks, width), bf16),
        in_specs=[VMEM, VMEM],
        out_specs=VMEM,
        compiler_params=PARAMS,
        cost_estimate=pl.CostEstimate(
            flops=2 * sources * blocks * table.size, bytes_accessed=4_000_000, transcendentals=0
        ),
        name="pick",
    )(table, ids)


def gather_kernel(ids_ref, slots_ref, *rest):
    acc_ref, out_ref = rest[:-1], rest[-1]
    names = out_ref.shape[0]
    rows = slots_ref.shape[0]
    piece = min(512, rows)
    total = acc_ref[0][...] if acc_ref else None
    name = lax.broadcasted_iota(jnp.int32, (names, piece), 0)
    for at in range(0, rows, piece):
        hot = jnp.where(name == ids_ref[:, at : at + piece], 1.0, 0.0).astype(bf16)
        part = mm(hot, slots_ref[at : at + piece, :])
        total = part if total is None else total + part
    out_ref[...] = total.astype(out_ref.dtype)


def gather(ids, slots, names, acc, dtype):
    width = slots.shape[1]
    return pl.pallas_call(
        gather_kernel,
        out_shape=jax.ShapeDtypeStruct((names, width), dtype),
        in_specs=[VMEM] * (2 + len(acc)),
        out_specs=VMEM,
        compiler_params=PARAMS,
        cost_estimate=pl.CostEstimate(
            flops=2 * slots.size * names, bytes_accessed=4_000_000, transcendentals=0
        ),
        name="gather",
    )(ids, slots, *acc)


def head_kernel(live, wq_t, wo, x_ref, c_ref, q_ref, d_ref):
    i = pl.program_id(0)
    pairs = q_ref.shape[0]
    for k in range(pairs):
        at = 2 * (pairs * i + k)
        q_ref[k] = mm_nt(wq_t[...], x_ref[2 * k : 2 * k + 2].reshape(2 * BT, D)).astype(bf16)
        cot = live_rows(c_ref[2 * k : 2 * k + 2].reshape(2 * BT, D), live[0, at], live[0, at + 1])
        d_ref[k] = mm_nt(wo[...], cot).astype(bf16)


def live_rows(cot, live0, live1):
    row = lax.broadcasted_iota(jnp.int32, (2 * BT, D), 0)
    kept = row < jnp.where(row < BT, live0, live1 + BT)
    return jnp.where(kept, cot.astype(f32), 0.0).astype(bf16)


def constant(shape):
    return pl.BlockSpec(shape, lambda i: (0,) * len(shape))


def project(live, wq_t, wo, x, cot):
    pairs = x.shape[0] // 2
    blocks = pl.BlockSpec((2 * PAIRS, BT, D), lambda i: (i, 0, 0))
    squares = pl.BlockSpec((PAIRS, D, 2 * BT), lambda i: (i, 0, 0))
    return pl.pallas_call(
        head_kernel,
        out_shape=(jax.ShapeDtypeStruct((pairs, D, 2 * BT), bf16),) * 2,
        grid=(pairs // PAIRS,),
        in_specs=[pl.BlockSpec(memory_space=pltpu.SMEM), constant((D, D)), constant((D, D))]
        + [blocks, blocks],
        out_specs=(squares, squares),
        compiler_params=PARAMS,
        cost_estimate=pl.CostEstimate(
            flops=8 * x.size * D, bytes_accessed=10 * x.size, transcendentals=0
        ),
        name="project",
    )(live, wq_t, wo, x, cot)


def tail_kernel(live, wq, wo_t, x_ref, c_ref, *rest):
    att_a, qg_a, att_b, qg_b, out_ref, tgrad_ref, grads_ref = rest
    i = pl.program_id(0)
    pairs = att_a.shape[0]

    @pl.when(i == 0)
    def _():
        grads_ref[...] = jnp.zeros_like(grads_ref)

    def work(att_ref, qg_ref):
        for k in range(pairs):
            at = 2 * (pairs * i + k)
            live0, live1 = live[0, at], live[0, at + 1]
            att, qg = att_ref[k], qg_ref[k]
            blocks = slice(2 * k, 2 * k + 2)
            lane = lax.broadcasted_iota(jnp.int32, (D, 2 * BT), 1)
            kept = lane < jnp.where(lane < BT, live0, live1 + BT)
            out = jnp.where(kept, mm(wo_t[...], att), 0.0)
            out_ref[blocks] = out.T.astype(bf16).reshape(2, BT, D)
            tgrad_ref[blocks] = mm(wq[...], qg).T.astype(bf16).reshape(2, BT, D)
            grads_ref[0:D] += mm(qg, x_ref[blocks].reshape(2 * BT, D))
            cot = live_rows(c_ref[blocks].reshape(2 * BT, D), live0, live1)
            grads_ref[D : 2 * D] += mm(att, cot)

    first = i < pl.num_programs(0) // 2

    @pl.when(first)
    def _():
        work(att_a, qg_a)

    @pl.when(jnp.logical_not(first))
    def _():
        work(att_b, qg_b)


def tokens_back(live, wq, wo_t, x, cot, halves):
    steps = x.shape[0] // 2 // PAIRS
    blocks = pl.BlockSpec((2 * PAIRS, BT, D), lambda i: (i, 0, 0))
    low = pl.BlockSpec((PAIRS, D, 2 * BT), lambda i: (jnp.minimum(i, steps // 2 - 1), 0, 0))
    high = pl.BlockSpec((PAIRS, D, 2 * BT), lambda i: (jnp.maximum(i - steps // 2, 0), 0, 0))
    tokens = jax.ShapeDtypeStruct(x.shape, bf16)
    return pl.pallas_call(
        tail_kernel,
        out_shape=(tokens, tokens, jax.ShapeDtypeStruct((2 * D, D), f32)),
        grid=(steps,),
        in_specs=[pl.BlockSpec(memory_space=pltpu.SMEM), constant((D, D)), constant((D, D))]
        + [blocks, blocks, low, low, high, high],
        out_specs=(blocks, blocks, constant((2 * D, D))),
        compiler_params=PARAMS,
        cost_estimate=pl.CostEstimate(
            flops=8 * x.size * D, bytes_accessed=12 * x.size, transcendentals=0
        ),
        name="tokens_back",
    )(live, wq, wo_t, x, cot, *halves)


def attend_kernel(base, wkv, wkv_t, grads_in, slots, queries, cot_grads, *rest):
    atts, qgs, hgrads, grads_ref = rest[:4]
    hbuf, qbuf, dbuf, abuf, tbuf, gbuf, kvs, kvts, kvg_s, in_sems, out_sems = rest[4:]
    steps = slots.shape[0] // 2
    slices = slots.shape[1]

    def loads(i):
        slot = lax.rem(i, 4)
        return [
            pltpu.make_async_copy(slots.at[pl.ds(2 * i, 2)], hbuf.at[slot], in_sems.at[slot, 0]),
            pltpu.make_async_copy(queries.at[base + i], qbuf.at[slot], in_sems.at[slot, 1]),
            pltpu.make_async_copy(cot_grads.at[base + i], dbuf.at[slot], in_sems.at[slot, 2]),
        ]

    def store_back(i):
        slot = lax.rem(i, 2)
        return pltpu.make_async_copy(
            gbuf.at[slot], hgrads.at[pl.ds(2 * i, 2)], out_sems.at[slot, 0]
        )

    def stores(i):
        slot = lax.rem(i, 2)
        return [
            pltpu.make_async_copy(abuf.at[slot], atts.at[i], out_sems.at[slot, 1]),
            pltpu.make_async_copy(tbuf.at[slot], qgs.at[i], out_sems.at[slot, 2]),
        ]

    zero = jnp.zeros((HD, BT), bf16)

    def paired(t, p):
        top = t[2 * HD * p : 2 * HD * p + HD]
        low = t[2 * HD * p + HD : 2 * HD * p + 2 * HD]
        return jnp.concatenate(
            [jnp.concatenate([top, zero], axis=1), jnp.concatenate([zero, low], axis=1)], axis=0
        )

    def cells(i):
        sliced = hbuf[lax.rem(i, 4)]
        return jnp.concatenate(
            [sliced[u, :, at : at + D] for u in range(2) for at in range(0, sliced.shape[2], D)],
            axis=0,
        )

    def head(i):
        slot = lax.rem(i, 2)

        def keys():
            kvs[slot] = mm(cells(i), wkv[...]).astype(bf16)

        def keys_t():
            kvts[slot] = mm_nt(wkv_t[...], cells(i)).astype(bf16)

        return [keys, keys_t]

    def tail(i):
        slot = lax.rem(i + 2, 2)

        def hidden_grad():
            back = mm(wkv[...], kvg_s[...]).astype(bf16)
            for u in range(2):
                gbuf[slot, u] = jnp.concatenate(
                    [back[at : at + slices, u * BT : u * BT + BT] for at in range(0, D, slices)],
                    axis=1,
                )

        def weight_grads():
            grads_ref[...] += mm(kvg_s[...], cells(i + 4))

        return [hidden_grad, weight_grads]

    def attention(i, between):
        slot = lax.rem(i, 2)
        kv, kv_t = kvs[slot], kvts[slot]
        q_t, d_t = qbuf[lax.rem(i, 4)], dbuf[lax.rem(i, 4)]
        att_rows, qg_rows, kg_rows, vg_rows = [[], []], [[], []], [[], []], [[], []]

        def first(p, u):
            rows = slice(u * BT, u * BT + BT)
            at = 2 * HD * p
            q2 = paired(q_t[:, rows], p)
            d2 = paired(d_t[:, rows], p)
            scores = mm(kv[rows, at : at + 2 * HD], q2)
            wg = mm(kv[rows, D + at : D + at + 2 * HD], d2)
            return q2, d2, scores, wg

        def second(q2, d2, scores, wg):
            top = jnp.max(scores, axis=0, keepdims=True)
            e = jnp.exp2((scores - top) * EXP2_SCALE)
            wf = e * (1.0 / jnp.sum(e, axis=0, keepdims=True))
            mean = jnp.sum(wf * wg, axis=0, keepdims=True)
            sg = (wf * (wg - mean)).astype(bf16)
            return q2, d2, wf.astype(bf16), sg

        def third(p, u, q2, d2, w, sg):
            rows = slice(u * BT, u * BT + BT)
            feats = slice(2 * HD * p, 2 * HD * p + 2 * HD)
            v_feats = slice(D + 2 * HD * p, D + 2 * HD * p + 2 * HD)
            att = mm(kv_t[v_feats, rows], w)
            att_rows[u] += [att[:HD, :BT], att[HD:, BT:]]
            qg = mm(kv_t[feats, rows], sg)
            qg_rows[u] += [qg[:HD, :BT], qg[HD:, BT:]]
            kg_rows[u].append(mm_nt(q2, sg) * SCALE)
            vg_rows[u].append(mm_nt(d2, w))

        units = [(p, u) for p in range(HEADS // 2) for u in range(2)]
        ready, soft = {}, {}
        between = list(between)
        for k in range(len(units) + AHEAD + 1):
            if k < len(units):
                ready[k] = first(*units[k])
            if between and k >= 1:
                between.pop(0)()
            j = k - AHEAD
            if 0 <= j < len(units):
                soft[j] = second(*ready.pop(j))
            if 0 <= j - 1 < len(units):
                third(*units[j - 1], *soft.pop(j - 1))
        for piece in between:
            piece()

        def joined(rows):
            return jnp.concatenate([jnp.concatenate(r, axis=0) for r in rows], axis=1)

        abuf[slot] = joined(att_rows).astype(bf16)
        tbuf[slot] = (joined(qg_rows) * SCALE).astype(bf16)
        kvg_s[...] = joined([kg_rows[u] + vg_rows[u] for u in range(2)]).astype(bf16)

    for c in loads(0) + loads(1):
        c.start()
    grads_ref[...] = grads_in[...]
    kvg_s[...] = jnp.zeros_like(kvg_s)
    hbuf[3] = jnp.zeros(hbuf.shape[1:], bf16)
    for c in loads(0):
        c.wait()
    for piece in head(0):
        piece()

    @pl.loop(0, steps)
    def _(i):
        @pl.when(i + 2 < steps)
        def _():
            for c in loads(i + 2):
                c.start()

        @pl.when(i + 1 < steps)
        def _():
            for c in loads(i + 1):
                c.wait()

        @pl.when(i >= 3)
        def _():
            store_back(i - 3).wait()

        @pl.when(i >= 2)
        def _():
            for c in stores(i - 2):
                c.wait()

        attention(i, [piece for two in zip(tail(i - 1), head(i + 1)) for piece in two])
        for c in stores(i):
            c.start()

        @pl.when(i >= 1)
        def _():
            store_back(i - 1).start()

    store_back(steps - 3).wait()
    for piece in tail(steps - 1):
        piece()
    store_back(steps - 1).start()
    for i in (steps - 2, steps - 1):
        store_back(i).wait()
        for c in stores(i):
            c.wait()


def attend(base, slots, queries, cot_grads, wkv, wkv_t, grads):
    steps = slots.shape[0] // 2
    square = jax.ShapeDtypeStruct((steps, D, 2 * BT), bf16)
    sliced = (2,) + slots.shape[1:]
    return pl.pallas_call(
        functools.partial(attend_kernel, base),
        out_shape=(
            square,
            square,
            jax.ShapeDtypeStruct(slots.shape, bf16),
            jax.ShapeDtypeStruct((2 * D, D), f32),
        ),
        in_specs=[VMEM] * 3 + [HBM] * 3,
        out_specs=(HBM, HBM, HBM, VMEM),
        scratch_shapes=[
            pltpu.VMEM((4,) + sliced, bf16),
            pltpu.VMEM((4, D, 2 * BT), bf16),
            pltpu.VMEM((4, D, 2 * BT), bf16),
            pltpu.VMEM((2, D, 2 * BT), bf16),
            pltpu.VMEM((2, D, 2 * BT), bf16),
            pltpu.VMEM((2,) + sliced, bf16),
            pltpu.VMEM((2, 2 * KEYS, 2 * D), bf16),
            pltpu.VMEM((2, 2 * D, 2 * KEYS), bf16),
            pltpu.VMEM((2 * D, 2 * KEYS), bf16),
            pltpu.SemaphoreType.DMA((4, 3)),
            pltpu.SemaphoreType.DMA((2, 3)),
        ],
        compiler_params=PARAMS,
        cost_estimate=pl.CostEstimate(
            flops=slots.shape[0] * 800_000_000,
            bytes_accessed=slots.shape[0] * 800_000,
            transcendentals=0,
        ),
        name="attend",
    )(wkv, wkv_t, grads, slots, queries, cot_grads)


def finish_kernel(slices_ref, shifts_ref, kv_grads, token_grads, hgrad_ref, sums_ref, back_t):
    slices = slices_ref.shape[1]
    used = 13 * D * D // LANES

    def put(k, grad):
        for j, at in enumerate(range(0, D, LANES)):
            row = (k * (D // LANES) + j) * D
            sums_ref[row : row + D] = grad[:, at : at + LANES].astype(bf16)

    put(0, token_grads[0:D])
    put(1, kv_grads[0:D])
    put(2, kv_grads[D : 2 * D])
    put(3, token_grads[D : 2 * D])
    if sums_ref.shape[0] > used:
        sums_ref[used:] = jnp.zeros((sums_ref.shape[0] - used, LANES), bf16)
    for s in range(SUB):
        cells = slice(s * KEYS, (s + 1) * KEYS)
        part = jnp.concatenate(
            [slices_ref[s, :, at : at + KEYS] for at in range(0, D * KEYS // slices, KEYS)], axis=0
        )
        back_t[:, cells] = part
        hgrad_ref[cells, :] = part.astype(f32).T.astype(bf16)
    for a in range(3):
        for b in range(3):
            put(4 + 3 * a + b, mm(back_t[...], shifts_ref[b, a * RX : a * RX + CELLS, :]))


def finish(slices, shifts, kv_grads, token_grads, rows):
    return pl.pallas_call(
        finish_kernel,
        out_shape=(
            jax.ShapeDtypeStruct((CELLS, D), bf16),
            jax.ShapeDtypeStruct((rows, LANES), bf16),
        ),
        in_specs=[VMEM] * 4,
        out_specs=(VMEM, VMEM),
        scratch_shapes=[pltpu.VMEM((D, CELLS), bf16)],
        compiler_params=PARAMS,
        cost_estimate=pl.CostEstimate(
            flops=2 * 9 * CELLS * D * D, bytes_accessed=6_000_000, transcendentals=0
        ),
        name="finish",
    )(slices, shifts, kv_grads, token_grads)


def normalize_kernel(sums_ref, query_ref, key_ref, value_ref, out_ref, conv_ref):
    def part(k):
        rows = [(k * (D // LANES) + j) * D for j in range(D // LANES)]
        return jnp.concatenate([sums_ref[r : r + D].astype(f32) for r in rows], axis=1)

    def squares(k):
        item = part(k)
        return jnp.sum(jnp.sum(item * item, axis=0, keepdims=True), axis=1, keepdims=True)

    def factor(total, size):
        return 1.0 / jnp.sqrt(total / size + EPSILON)

    for k, ref in enumerate((query_ref, key_ref, value_ref)):
        ref[...] = (part(k) * factor(squares(k), D * D)).T
    out_ref[...] = part(3) * factor(squares(3), D * D)
    total = squares(4)
    for k in range(5, 13):
        total = total + squares(k)
    scale = factor(total, 9 * D * D)
    for k in range(9):
        conv_ref[k] = (part(4 + k) * scale).T


def normalize(sums):
    square = jax.ShapeDtypeStruct((D, D), f32)
    return pl.pallas_call(
        normalize_kernel,
        out_shape=(square,) * 4 + (jax.ShapeDtypeStruct((9, D, D), f32),),
        in_specs=[pl.BlockSpec(memory_space=pltpu.VMEM)],
        out_specs=(pl.BlockSpec(memory_space=pltpu.VMEM),) * 5,
        compiler_params=pltpu.CompilerParams(vmem_limit_bytes=60 * 1024 * 1024),
        cost_estimate=pl.CostEstimate(flops=4_000_000, bytes_accessed=6_000_000, transcendentals=0),
        name="normalize",
    )(sums)


def ring(value, by):
    length = lax.axis_size("tile")
    return lax.ppermute(value, "tile", [(i, (i + by) % length) for i in range(length)])


def turned(row, flag):
    return jnp.where(flag == 1, row[::-1], row)


def exchange(value, axes="tile"):
    return lax.all_to_all(value, axes, split_axis=0, concat_axis=0, tiled=True)


def local(
    grid,
    tokens,
    targets,
    sub_masks,
    live_counts,
    edge_turns,
    w_query,
    w_key,
    w_value,
    w_out,
    w_conv,
    token_cotan,
):
    ntile = lax.axis_size("tile")
    ndev = ntile * lax.axis_size("win")
    turns = edge_turns[0]
    nblocks = tokens.shape[1] // BT

    sub = jnp.sum(sub_masks[0] * jnp.arange(SUB, dtype=jnp.int32)[None, :], axis=1)
    names = jnp.concatenate([targets[0, :, 0], sub]).astype(bf16)
    names = jnp.pad(names[None], ((0, SUB - 1), (0, 0)))

    field = grid[0]
    above = turned(ring(field[-1], 1), turns[0])
    below = turned(ring(field[0], -1), turns[1])
    rimmed = jnp.concatenate([above[None], field, below[None]], axis=0).reshape(-1, D)
    sliced, shifts = hidden_slices(rimmed, w_conv.reshape(9, D, D), ntile)
    width = sliced.shape[2]
    sliced = jnp.concatenate(
        [sliced.transpose(1, 0, 2), jnp.broadcast_to(names[None], (ntile,) + names.shape)], axis=2
    )
    table = exchange(sliced)
    ids = table[:, 0, width:].astype(jnp.int32)
    ids = ids[:, :nblocks] * SUB + ids[:, nblocks:]
    table = table.reshape(ntile * SUB, -1)

    wkv = jnp.concatenate([w_key, w_value], axis=1)
    x = tokens[0].reshape(nblocks, BT, D)
    cot = token_cotan[0].reshape(nblocks, BT, D)
    half = nblocks // 2
    queries, cot_grads = project(live_counts, w_query.T, w_out, x, cot)
    grads = jnp.zeros((2 * D, D), f32)
    got = [exchange(pick(table, ids[:, c * half : (c + 1) * half].T, width)) for c in range(2)]
    halves, returned = [], []
    for c in range(2):
        att, query_grad, back, grads = attend(
            c * half // 2, got[c].transpose(1, 0, 2), queries, cot_grads, wkv, wkv.T, grads
        )
        halves += [att, query_grad]
        returned.append(exchange(back.transpose(1, 0, 2)).reshape(ntile * half, -1))
    token_out, token_grad, token_grads = tokens_back(
        live_counts, w_query, w_out.T, x, cot, halves
    )
    rows = [ids[:, c * half : (c + 1) * half].reshape(1, -1) for c in range(2)]
    acc = gather(rows[0], returned[0], ntile * SUB, (), f32)
    home = gather(rows[1], returned[1], ntile * SUB, (acc,), bf16)
    home = exchange(home.reshape(ntile, SUB, -1)).transpose(1, 0, 2)
    each = -(-13 * D * D // LANES // (8 * ndev)) * 8
    hidden_back, sums = finish(home, shifts, grads, token_grads, ndev * each)

    parts = exchange(sums.reshape(ndev, -1, LANES), ("tile", "win"))
    share = jnp.sum(parts.astype(f32), axis=0).astype(bf16)

    hidden_back = hidden_back.reshape(RY, RX, D)
    padded = jnp.pad(hidden_back, ((0, 0), (1, 1), (0, 0)))
    taps = []
    for a in range(3):
        piece = jnp.zeros((RY, RX, D), f32)
        for b in range(3):
            cells = padded[:, 2 - b : 2 - b + RX].reshape(-1, D)
            piece = piece + mm_nt(cells, w_conv[a, b]).reshape(RY, RX, D)
        taps.append(piece)
    from_below = ring(turned(taps[0][0], turns[0]), -1)
    from_above = ring(turned(taps[2][-1], turns[1]), 1)
    field_grad = hidden_back.astype(f32) + taps[1]
    field_grad = field_grad + jnp.concatenate([taps[0][1:], from_below[None]], axis=0)
    field_grad = field_grad + jnp.concatenate([from_above[None], taps[2][:-1]], axis=0)
    grid_grad = field_grad.astype(bf16)[None]
    share, grid_grad = lax.optimization_barrier((share, grid_grad))
    spread = jnp.broadcast_to(share[None], (ndev,) + share.shape)
    updates = normalize(exchange(spread, ("tile", "win")).reshape(-1, LANES))

    return (
        token_out.reshape(1, -1, D),
        token_grad.reshape(1, -1, D),
        grid_grad,
        *updates[:4],
        updates[4].reshape(3, 3, D, D),
    )


def solution(mesh):
    return jax.shard_map(
        local,
        mesh=mesh,
        in_specs=(
            P("win", "tile", None, None),
            P("win", "tile", None),
            P("win", "tile", None),
            P("win", "tile", None),
            P("win", "tile"),
            P("tile", None),
            P(),
            P(),
            P(),
            P(),
            P(),
            P("win", "tile", None),
        ),
        out_specs=(
            P("win", "tile", None),
            P("win", "tile", None),
            P("win", "tile", None, None),
            P(),
            P(),
            P(),
            P(),
            P(),
        ),
        check_vma=False,
    )
```

```python
import functools
import math

import jax
import jax.numpy as jnp
from jax import lax
from jax.experimental import pallas as pl
from jax.experimental.pallas import tpu as pltpu
from jax.sharding import PartitionSpec as P

D = 256
HEADS = 8
HD = 32
BT = 128
RY = 32
RX = 32
SUB = 8
LANES = 128
KEYS = 128
CELLS = RY * RX
EPSILON = 1e-06
SCALE = 1.0 / math.sqrt(HD)
EXP2_SCALE = SCALE * math.log2(math.e)
AHEAD = 3

f32 = jnp.float32
bf16 = jnp.bfloat16


def mm(a, b):
    return lax.dot_general(a, b, (((1,), (0,)), ((), ())), preferred_element_type=f32)


def mm_nt(a, b):
    return lax.dot_general(a, b, (((1,), (1,)), ((), ())), preferred_element_type=f32)


VMEM = pl.BlockSpec(memory_space=pltpu.VMEM)
HBM = pl.BlockSpec(memory_space=pltpu.HBM)
PARAMS = pltpu.CompilerParams(vmem_limit_bytes=60 * 1024 * 1024)


def hidden_kernel(rim_ref, w_ref, send_ref, shifts_ref):
    rim = rim_ref[...].astype(f32)
    rows = rim.shape[0]
    col = lax.broadcasted_iota(jnp.int32, (rows, D), 0) % RX
    shifts_ref[0] = jnp.where(col == 0, 0.0, pltpu.roll(rim, 1, 0)).astype(bf16)
    shifts_ref[1] = rim_ref[...]
    shifts_ref[2] = jnp.where(col == RX - 1, 0.0, pltpu.roll(rim, rows - 1, 0)).astype(bf16)
    slices = send_ref.shape[1]
    piece = CELLS // 4

    @pl.loop(0, 4)
    def _(i):
        base = i * piece
        total = rim_ref[pl.ds(pl.multiple_of(base + RX, RX), piece), :].astype(f32)
        for a in range(3):
            for b in range(3):
                cells = shifts_ref[b, pl.ds(pl.multiple_of(base + a * RX, RX), piece), :]
                total = total + mm(cells, w_ref[3 * a + b])
        hidden = total.astype(bf16)
        for k in range(piece // KEYS):
            cuts = range(k * KEYS, (k + 1) * KEYS, slices)
            send_ref[i * (piece // KEYS) + k] = jnp.concatenate(
                [hidden[at : at + slices] for at in cuts], axis=1
            )


def hidden_slices(rimmed, w_conv, slices):
    rows = (RY + 2) * RX
    return pl.pallas_call(
        hidden_kernel,
        out_shape=(
            jax.ShapeDtypeStruct((SUB, slices, KEYS * D // slices), bf16),
            jax.ShapeDtypeStruct((3, rows, D), bf16),
        ),
        in_specs=[VMEM, VMEM],
        out_specs=(VMEM, VMEM),
        compiler_params=PARAMS,
        cost_estimate=pl.CostEstimate(
            flops=2 * 9 * CELLS * D * D, bytes_accessed=6_000_000, transcendentals=0
        ),
        name="conv_slices",
    )(rimmed, w_conv)


def pick_kernel(table_ref, ids_ref, out_ref):
    names = table_ref.shape[0]
    width = out_ref.shape[2]
    blocks, sources = ids_ref.shape
    group = 256 // blocks
    lane = lax.broadcasted_iota(jnp.int32, (blocks, names), 1)
    for g in range(0, sources, group):
        hot = [
            jnp.where(lane == ids_ref[:, g + k : g + k + 1], 1.0, 0.0).astype(bf16)
            for k in range(group)
        ]
        rows = mm(jnp.concatenate(hot, axis=0), table_ref[:, :width]).astype(bf16)
        for k in range(group):
            out_ref[g + k] = rows[k * blocks : (k + 1) * blocks]


def pick(table, ids, width):
    blocks, sources = ids.shape
    return pl.pallas_call(
        pick_kernel,
        out_shape=jax.ShapeDtypeStruct((sources, blocks, width), bf16),
        in_specs=[VMEM, VMEM],
        out_specs=VMEM,
        compiler_params=PARAMS,
        cost_estimate=pl.CostEstimate(
            flops=2 * sources * blocks * table.size, bytes_accessed=4_000_000, transcendentals=0
        ),
        name="pick",
    )(table, ids)


def gather_kernel(ids_ref, slots_ref, *rest):
    acc_ref, out_ref = rest[:-1], rest[-1]
    names = out_ref.shape[0]
    rows = slots_ref.shape[0]
    piece = min(512, rows)
    total = acc_ref[0][...] if acc_ref else None
    name = lax.broadcasted_iota(jnp.int32, (names, piece), 0)
    for at in range(0, rows, piece):
        hot = jnp.where(name == ids_ref[:, at : at + piece], 1.0, 0.0).astype(bf16)
        part = mm(hot, slots_ref[at : at + piece, :])
        total = part if total is None else total + part
    out_ref[...] = total.astype(out_ref.dtype)


def gather(ids, slots, names, acc, dtype):
    width = slots.shape[1]
    return pl.pallas_call(
        gather_kernel,
        out_shape=jax.ShapeDtypeStruct((names, width), dtype),
        in_specs=[VMEM] * (2 + len(acc)),
        out_specs=VMEM,
        compiler_params=PARAMS,
        cost_estimate=pl.CostEstimate(
            flops=2 * slots.size * names, bytes_accessed=4_000_000, transcendentals=0
        ),
        name="gather",
    )(ids, slots, *acc)


def attend_kernel(base, live, wq, wq_t, wkv, wkv_t, wo, wo_t, grads_in, slots, xs, cots, *rest):
    outs, tgrads, hgrads, grads_ref = rest[-19:-15]
    hbuf, xbuf, cbuf, obuf, tbuf, gbuf = rest[-15:-9]
    kvs, kvts, qts, dts, att_s, qg_s, kvg_s, in_sems, out_sems = rest[-9:]
    steps = slots.shape[0] // 2
    slices = slots.shape[1]

    def loads(i):
        blocks = pl.ds(base + 2 * i, 2)
        slot = lax.rem(i, 4)
        return [
            pltpu.make_async_copy(slots.at[pl.ds(2 * i, 2)], hbuf.at[slot], in_sems.at[slot, 0]),
            pltpu.make_async_copy(xs.at[blocks], xbuf.at[slot], in_sems.at[slot, 1]),
            pltpu.make_async_copy(cots.at[blocks], cbuf.at[slot], in_sems.at[slot, 2]),
        ]

    def stores(i):
        blocks = pl.ds(base + 2 * i, 2)
        slot = lax.rem(i, 2)
        return [
            pltpu.make_async_copy(gbuf.at[slot], hgrads.at[pl.ds(2 * i, 2)], out_sems.at[slot, 0]),
            pltpu.make_async_copy(obuf.at[slot], outs.at[blocks], out_sems.at[slot, 1]),
            pltpu.make_async_copy(tbuf.at[slot], tgrads.at[blocks], out_sems.at[slot, 2]),
        ]

    zero = jnp.zeros((HD, BT), bf16)

    def paired(t, p):
        top = t[2 * HD * p : 2 * HD * p + HD]
        low = t[2 * HD * p + HD : 2 * HD * p + 2 * HD]
        return jnp.concatenate(
            [jnp.concatenate([top, zero], axis=1), jnp.concatenate([zero, low], axis=1)], axis=0
        )

    def lives(i):
        at = base + 2 * jnp.minimum(i, steps - 1)
        return live[0, at], live[0, at + 1]

    def cells(i):
        sliced = hbuf[lax.rem(i, 4)]
        return jnp.concatenate(
            [sliced[u, :, at : at + D] for u in range(2) for at in range(0, sliced.shape[2], D)],
            axis=0,
        )

    def rows_of(buf, i):
        return buf[lax.rem(i, 4)].reshape(2 * BT, D)

    def head(i):
        slot = lax.rem(i, 2)

        def keys():
            kvs[slot] = mm(cells(i), wkv[...]).astype(bf16)

        def keys_t():
            kvts[slot] = mm_nt(wkv_t[...], cells(i)).astype(bf16)

        def queries():
            qts[slot] = mm_nt(wq_t[...], rows_of(xbuf, i)).astype(bf16)

        def cotangents():
            live0, live1 = lives(i)
            row = lax.broadcasted_iota(jnp.int32, (2 * BT, D), 0)
            row_live = row < jnp.where(row < BT, live0, live1 + BT)
            cot = jnp.where(row_live, rows_of(cbuf, i).astype(f32), 0.0).astype(bf16)
            cbuf[lax.rem(i, 4)] = cot.reshape(2, BT, D)
            dts[slot] = mm_nt(wo[...], cot).astype(bf16)

        return [cotangents, queries, keys, keys_t]

    def tail(i):
        slot = lax.rem(i + 2, 2)

        def mixed():
            live0, live1 = lives(i)
            lane = lax.broadcasted_iota(jnp.int32, (D, 2 * BT), 1)
            lane_live = lane < jnp.where(lane < BT, live0, live1 + BT)
            out = jnp.where(lane_live, mm(wo_t[...], att_s[...]), 0.0)
            obuf[slot] = out.T.astype(bf16).reshape(2, BT, D)

        def token_grad():
            tbuf[slot] = mm(wq[...], qg_s[...]).T.astype(bf16).reshape(2, BT, D)

        def hidden_grad():
            back = mm(wkv[...], kvg_s[...]).astype(bf16)
            for u in range(2):
                gbuf[slot, u] = jnp.concatenate(
                    [back[at : at + slices, u * BT : u * BT + BT] for at in range(0, D, slices)],
                    axis=1,
                )

        def weight_grads():
            grads_ref[0:256] += mm(qg_s[...], rows_of(xbuf, i + 4))
            grads_ref[256:768] += mm(kvg_s[...], cells(i + 4))
            grads_ref[768:1024] += mm(att_s[...], rows_of(cbuf, i + 4))

        return [hidden_grad, mixed, token_grad, weight_grads]

    def attention(i, between):
        slot = lax.rem(i, 2)
        kv, kv_t, q_t, d_t = kvs[slot], kvts[slot], qts[slot], dts[slot]
        att_rows, qg_rows, kg_rows, vg_rows = [[], []], [[], []], [[], []], [[], []]

        def first(p, u):
            rows = slice(u * BT, u * BT + BT)
            at = 2 * HD * p
            q2 = paired(q_t[:, rows], p)
            d2 = paired(d_t[:, rows], p)
            scores = mm(kv[rows, at : at + 2 * HD], q2)
            wg = mm(kv[rows, D + at : D + at + 2 * HD], d2)
            return q2, d2, scores, wg

        def second(q2, d2, scores, wg):
            top = jnp.max(scores, axis=0, keepdims=True)
            e = jnp.exp2((scores - top) * EXP2_SCALE)
            wf = e * (1.0 / jnp.sum(e, axis=0, keepdims=True))
            mean = jnp.sum(wf * wg, axis=0, keepdims=True)
            sg = (wf * (wg - mean)).astype(bf16)
            return q2, d2, wf.astype(bf16), sg

        def third(p, u, q2, d2, w, sg):
            rows = slice(u * BT, u * BT + BT)
            feats = slice(2 * HD * p, 2 * HD * p + 2 * HD)
            v_feats = slice(D + 2 * HD * p, D + 2 * HD * p + 2 * HD)
            att = mm(kv_t[v_feats, rows], w)
            att_rows[u] += [att[:HD, :BT], att[HD:, BT:]]
            qg = mm(kv_t[feats, rows], sg)
            qg_rows[u] += [qg[:HD, :BT], qg[HD:, BT:]]
            kg_rows[u].append(mm_nt(q2, sg) * SCALE)
            vg_rows[u].append(mm_nt(d2, w))

        units = [(p, u) for p in range(HEADS // 2) for u in range(2)]
        ready, soft = {}, {}
        between = list(between)
        for k in range(len(units) + AHEAD + 1):
            if k < len(units):
                ready[k] = first(*units[k])
            if between and k >= 1:
                between.pop(0)()
            j = k - AHEAD
            if 0 <= j < len(units):
                soft[j] = second(*ready.pop(j))
            if 0 <= j - 1 < len(units):
                third(*units[j - 1], *soft.pop(j - 1))
        for piece in between:
            piece()

        def joined(rows):
            return jnp.concatenate([jnp.concatenate(r, axis=0) for r in rows], axis=1)

        att_s[...] = joined(att_rows).astype(bf16)
        qg_s[...] = (joined(qg_rows) * SCALE).astype(bf16)
        kvg_s[...] = joined([kg_rows[u] + vg_rows[u] for u in range(2)]).astype(bf16)

    for c in loads(0):
        c.start()
    for c in loads(1):
        c.start()
    grads_ref[...] = grads_in[...]
    for ref in (att_s, qg_s, kvg_s):
        ref[...] = jnp.zeros_like(ref)
    for ref in (hbuf, xbuf, cbuf):
        ref[3] = jnp.zeros(ref.shape[1:], bf16)
    for c in loads(0):
        c.wait()
    for piece in head(0):
        piece()

    @pl.loop(0, steps)
    def _(i):
        @pl.when(i + 2 < steps)
        def _():
            for c in loads(i + 2):
                c.start()

        @pl.when(i + 1 < steps)
        def _():
            for c in loads(i + 1):
                c.wait()

        @pl.when(i >= 3)
        def _():
            for c in stores(i - 3):
                c.wait()

        attention(i, [piece for two in zip(tail(i - 1), head(i + 1)) for piece in two])

        @pl.when(i >= 1)
        def _():
            for c in stores(i - 1):
                c.start()

    for c in stores(steps - 3):
        c.wait()
    for piece in tail(steps - 1):
        piece()
    for c in stores(steps - 1):
        c.start()
    for i in (steps - 2, steps - 1):
        for c in stores(i):
            c.wait()


def attend(base, live, slots, x, cot, weights, grads, kept):
    args = [live, *weights, grads, slots, x, cot, *kept]
    first_kept = len(args) - len(kept)
    token_shape = jax.ShapeDtypeStruct(x.shape, bf16)
    return pl.pallas_call(
        functools.partial(attend_kernel, base),
        out_shape=(
            token_shape,
            token_shape,
            jax.ShapeDtypeStruct(slots.shape, bf16),
            jax.ShapeDtypeStruct((4 * D, D), f32),
        ),
        in_specs=[pl.BlockSpec(memory_space=pltpu.SMEM)]
        + [VMEM] * (len(weights) + 1)
        + [HBM] * (3 + len(kept)),
        out_specs=(HBM, HBM, HBM, VMEM),
        scratch_shapes=[
            pltpu.VMEM((4, 2) + slots.shape[1:], bf16),
            pltpu.VMEM((4, 2, BT, D), bf16),
            pltpu.VMEM((4, 2, BT, D), bf16),
            pltpu.VMEM((2, 2, BT, D), bf16),
            pltpu.VMEM((2, 2, BT, D), bf16),
            pltpu.VMEM((2, 2) + slots.shape[1:], bf16),
            pltpu.VMEM((2, 2 * KEYS, 2 * D), bf16),
            pltpu.VMEM((2, 2 * D, 2 * KEYS), bf16),
            pltpu.VMEM((2, D, 2 * BT), bf16),
            pltpu.VMEM((2, D, 2 * BT), bf16),
            pltpu.VMEM((D, 2 * BT), bf16),
            pltpu.VMEM((D, 2 * BT), bf16),
            pltpu.VMEM((2 * D, 2 * KEYS), bf16),
            pltpu.SemaphoreType.DMA((4, 3)),
            pltpu.SemaphoreType.DMA((2, 3)),
        ],
        input_output_aliases={first_kept + j: j for j in range(len(kept))},
        compiler_params=PARAMS,
        cost_estimate=pl.CostEstimate(
            flops=slots.shape[0] * 800_000_000,
            bytes_accessed=slots.shape[0] * 800_000,
            transcendentals=0,
        ),
        name="attend",
    )(*args)


def finish_kernel(slices_ref, shifts_ref, grads_ref, hgrad_ref, sums_ref, back_t):
    slices = slices_ref.shape[1]
    used = 13 * D * D // LANES

    def put(k, grad):
        for j, at in enumerate(range(0, D, LANES)):
            row = (k * (D // LANES) + j) * D
            sums_ref[row : row + D] = grad[:, at : at + LANES].astype(bf16)

    for k in range(4):
        put(k, grads_ref[k * D : (k + 1) * D])
    if sums_ref.shape[0] > used:
        sums_ref[used:] = jnp.zeros((sums_ref.shape[0] - used, LANES), bf16)
    for s in range(SUB):
        cells = slice(s * KEYS, (s + 1) * KEYS)
        part = jnp.concatenate(
            [slices_ref[s, :, at : at + KEYS] for at in range(0, D * KEYS // slices, KEYS)], axis=0
        )
        back_t[:, cells] = part
        hgrad_ref[cells, :] = part.astype(f32).T.astype(bf16)
    for a in range(3):
        for b in range(3):
            put(4 + 3 * a + b, mm(back_t[...], shifts_ref[b, a * RX : a * RX + CELLS, :]))


def finish(slices, shifts, grads, rows):
    return pl.pallas_call(
        finish_kernel,
        out_shape=(
            jax.ShapeDtypeStruct((CELLS, D), bf16),
            jax.ShapeDtypeStruct((rows, LANES), bf16),
        ),
        in_specs=[VMEM] * 3,
        out_specs=(VMEM, VMEM),
        scratch_shapes=[pltpu.VMEM((D, CELLS), bf16)],
        compiler_params=PARAMS,
        cost_estimate=pl.CostEstimate(
            flops=2 * 9 * CELLS * D * D, bytes_accessed=6_000_000, transcendentals=0
        ),
        name="finish",
    )(slices, shifts, grads)


def normalize_kernel(sums_ref, query_ref, key_ref, value_ref, out_ref, conv_ref):
    def part(k):
        rows = [(k * (D // LANES) + j) * D for j in range(D // LANES)]
        return jnp.concatenate([sums_ref[r : r + D].astype(f32) for r in rows], axis=1)

    def squares(k):
        item = part(k)
        return jnp.sum(jnp.sum(item * item, axis=0, keepdims=True), axis=1, keepdims=True)

    def factor(total, size):
        return 1.0 / jnp.sqrt(total / size + EPSILON)

    for k, ref in enumerate((query_ref, key_ref, value_ref)):
        ref[...] = (part(k) * factor(squares(k), D * D)).T
    out_ref[...] = part(3) * factor(squares(3), D * D)
    total = squares(4)
    for k in range(5, 13):
        total = total + squares(k)
    scale = factor(total, 9 * D * D)
    for k in range(9):
        conv_ref[k] = (part(4 + k) * scale).T


def normalize(sums):
    square = jax.ShapeDtypeStruct((D, D), f32)
    return pl.pallas_call(
        normalize_kernel,
        out_shape=(square,) * 4 + (jax.ShapeDtypeStruct((9, D, D), f32),),
        in_specs=[pl.BlockSpec(memory_space=pltpu.VMEM)],
        out_specs=(pl.BlockSpec(memory_space=pltpu.VMEM),) * 5,
        compiler_params=pltpu.CompilerParams(vmem_limit_bytes=60 * 1024 * 1024),
        cost_estimate=pl.CostEstimate(flops=4_000_000, bytes_accessed=6_000_000, transcendentals=0),
        name="normalize",
    )(sums)


def ring(value, by):
    length = lax.axis_size("tile")
    return lax.ppermute(value, "tile", [(i, (i + by) % length) for i in range(length)])


def turned(row, flag):
    return jnp.where(flag == 1, row[::-1], row)


def exchange(value, axes="tile"):
    return lax.all_to_all(value, axes, split_axis=0, concat_axis=0, tiled=True)


def local(
    grid,
    tokens,
    targets,
    sub_masks,
    live_counts,
    edge_turns,
    w_query,
    w_key,
    w_value,
    w_out,
    w_conv,
    token_cotan,
):
    ntile = lax.axis_size("tile")
    ndev = ntile * lax.axis_size("win")
    turns = edge_turns[0]
    nblocks = tokens.shape[1] // BT

    sub = jnp.sum(sub_masks[0] * jnp.arange(SUB, dtype=jnp.int32)[None, :], axis=1)
    names = jnp.concatenate([targets[0, :, 0], sub]).astype(bf16)
    names = jnp.pad(names[None], ((0, SUB - 1), (0, 0)))

    field = grid[0]
    above = turned(ring(field[-1], 1), turns[0])
    below = turned(ring(field[0], -1), turns[1])
    rimmed = jnp.concatenate([above[None], field, below[None]], axis=0).reshape(-1, D)
    sliced, shifts = hidden_slices(rimmed, w_conv.reshape(9, D, D), ntile)
    width = sliced.shape[2]
    sliced = jnp.concatenate(
        [sliced.transpose(1, 0, 2), jnp.broadcast_to(names[None], (ntile,) + names.shape)], axis=2
    )
    table = exchange(sliced)
    ids = table[:, 0, width:].astype(jnp.int32)
    ids = ids[:, :nblocks] * SUB + ids[:, nblocks:]
    table = table.reshape(ntile * SUB, -1)

    wkv = jnp.concatenate([w_key, w_value], axis=1)
    weights = (w_query, w_query.T, wkv, wkv.T, w_out, w_out.T)
    x = tokens[0].reshape(nblocks, BT, D)
    cot = token_cotan[0].reshape(nblocks, BT, D)
    half = nblocks // 2
    grads = jnp.zeros((4 * D, D), f32)
    got = [exchange(pick(table, ids[:, c * half : (c + 1) * half].T, width)) for c in range(2)]
    kept, returned = (), []
    for c in range(2):
        token_out, token_grad, back, grads = attend(
            c * half, live_counts, got[c].transpose(1, 0, 2), x, cot, weights, grads, kept
        )
        kept = (token_out, token_grad)
        returned.append(exchange(back.transpose(1, 0, 2)).reshape(ntile * half, -1))
    rows = [ids[:, c * half : (c + 1) * half].reshape(1, -1) for c in range(2)]
    acc = gather(rows[0], returned[0], ntile * SUB, (), f32)
    home = gather(rows[1], returned[1], ntile * SUB, (acc,), bf16)
    home = exchange(home.reshape(ntile, SUB, -1)).transpose(1, 0, 2)
    each = -(-13 * D * D // LANES // (8 * ndev)) * 8
    hidden_back, sums = finish(home, shifts, grads, ndev * each)

    parts = exchange(sums.reshape(ndev, -1, LANES), ("tile", "win"))
    share = jnp.sum(parts.astype(f32), axis=0).astype(bf16)

    hidden_back = hidden_back.reshape(RY, RX, D)
    padded = jnp.pad(hidden_back, ((0, 0), (1, 1), (0, 0)))
    taps = []
    for a in range(3):
        piece = jnp.zeros((RY, RX, D), f32)
        for b in range(3):
            cells = padded[:, 2 - b : 2 - b + RX].reshape(-1, D)
            piece = piece + mm_nt(cells, w_conv[a, b]).reshape(RY, RX, D)
        taps.append(piece)
    from_below = ring(turned(taps[0][0], turns[0]), -1)
    from_above = ring(turned(taps[2][-1], turns[1]), 1)
    share, from_below, from_above = lax.optimization_barrier((share, from_below, from_above))
    field_grad = hidden_back.astype(f32) + taps[1]
    field_grad = field_grad + jnp.concatenate([taps[0][1:], from_below[None]], axis=0)
    field_grad = field_grad + jnp.concatenate([from_above[None], taps[2][:-1]], axis=0)
    grid_grad = field_grad.astype(bf16)[None]
    spread = jnp.broadcast_to(share[None], (ndev,) + share.shape)
    updates = normalize(exchange(spread, ("tile", "win")).reshape(-1, LANES))

    return (
        token_out.reshape(1, -1, D),
        token_grad.reshape(1, -1, D),
        grid_grad,
        *updates[:4],
        updates[4].reshape(3, 3, D, D),
    )


def solution(mesh):
    return jax.shard_map(
        local,
        mesh=mesh,
        in_specs=(
            P("win", "tile", None, None),
            P("win", "tile", None),
            P("win", "tile", None),
            P("win", "tile", None),
            P("win", "tile"),
            P("tile", None),
            P(),
            P(),
            P(),
            P(),
            P(),
            P("win", "tile", None),
        ),
        out_specs=(
            P("win", "tile", None),
            P("win", "tile", None),
            P("win", "tile", None, None),
            P(),
            P(),
            P(),
            P(),
            P(),
        ),
        check_vma=False,
    )
```
